128 devices in a mesh: dp: 4 (over z), expert: 32 (over x, y, core).
Axes of the slice: x: 4, y: 4, z: 4, core: 2. Of those that a mesh axis runs over, the one named last changes fastest.
Arguments:
- hidden: bfloat16 [12288, 2880], P('expert', 'dp'), may hold values from -6 to 6
- segments: int32 [32, 384], P('expert'), may hold values from 0 to 3, never falling along the last dimension, each value on 1 to 192 neighbouring positions
- request_adapter: int32 [32, 4], P('expert'), may hold values from 0 to 7
- routes: int32 [32, 384, 4], P('expert', 'dp'), may hold values from 0 to 31, all different within a row; in each aligned block of 96 rows (0 to 95, 96 to 191, ..., all dimensions but the last counted through in order) at most 16 rows name the same one
- expert_gates: bfloat16 [32, 384, 4], P('expert', 'dp'), may hold values from 0.049804688 to 0.59765625
- attention_gain: float32 [2880], replicated, may hold values from 0.25 to 1.75
- joined_weight: bfloat16 [2880, 4, 640], P(None, 'dp'), may hold values from -0.109375 to 0.109375
- sinks: float32 [32], P('dp'), may hold values from 0 to 3
- attention_out_weight: bfloat16 [2048, 2880], P('dp'), may hold values from -0.125 to 0.125
- joined_down_maps: bfloat16 [2880, 128], replicated, may hold values from -0.109375 to 0.109375
- joined_up_maps: bfloat16 [128, 4, 640], P(None, 'dp'), may hold values from -0.375 to 0.375
- output_down_maps: bfloat16 [2048, 128], P('dp'), may hold values from -0.125 to 0.125
- output_up_maps: bfloat16 [128, 2880], P(None, 'dp'), may hold values from -0.75 to 0.75
- expert_norm_gain: float32 [2880], replicated, may hold values from 0.25 to 1.75
- expert_gate_weight: bfloat16 [32, 2880, 2880], P('expert', None, 'dp'), may hold values from -0.109375 to 0.109375
- expert_up_weight: bfloat16 [32, 2880, 2880], P('expert', None, 'dp'), may hold values from -0.109375 to 0.109375
- expert_down_weight: bfloat16 [32, 2880, 2880], P('expert', 'dp'), may hold values from -0.109375 to 0.109375
- closing_gain: float32 [2880], replicated, may hold values from 0.25 to 1.75
- vocabulary_weight: bfloat16 [2880, 102400], P(None, ('dp', 'expert')), may hold values from -0.109375 to 0.109375
Outputs:
- hidden_out: bfloat16 [12288, 2880], P('expert', 'dp')
- logits: float32 [128, 102400], P(None, ('dp', 'expert'))
The draws below stay inside these ranges and needn't reach their ends.
Inputs may be any that keep to these rules, and one draw needn't show every extreme that they name: `segments`: in each column the ids do not fall; each of the 4 requests has 1 to 192 tokens, and one has exactly 192. `routes`: the 4 experts of a token differ. Within the rows of one device (96 consecutive tokens, aligned blocks) no expert is named more than 16 times, and in some blocks one expert is named exactly 16 times.
All inputs are finite; a program needn't handle non-finite values.
Results may differ from the reference program's by a relative error of at most 0.02.
Values may be sent and summed in bfloat16 or wider, within the bound.
A program may use at most 128 MiB of HBM per device.

```python
import math
import jax
import jax.numpy as jnp
import numpy as np
from jax import lax

MODEL_WIDTH = 2880
HEAD_SIZE = 64
QUERY_GROUP = 8
KEY_VALUE_HEADS = 4
QUERY_HEADS = 32
FF = 2880
EXPERTS = 32
TOP = 4
ADAPTER_RANK = 16
ADAPTER_COUNT = 8
TOK_DEV = 96
TOK_COL = 384
COLUMNS = 32
TOKENS = 12288
REQS = 4
MAX_LEN = 192
CAP = 16
LAST = 128
VOCAB = 102400
N_DP = 4


def plant(drawn, key, low, high):
    longest = drawn.shape.index(max(drawn.shape))
    spots = []
    for shift in (0, 1):
        where = [jax.random.randint(jax.random.fold_in(key, axis), (), 0, length) for axis, length in enumerate(drawn.shape)]
        where[longest] = (where[longest] + shift) % drawn.shape[longest]
        spots.append(tuple(where))
    return drawn.at[spots[0]].set(low).at[spots[1]].set(high)


def steps_of(key, shape, split, smallest, largest):
    def one(dim, shards_of):
        steps = jax.random.uniform(jax.random.fold_in(jax.random.fold_in(key, 6), dim), (shards_of,), jnp.float32, smallest / len(split), largest / len(split))
        return jnp.repeat(jnp.exp(steps), shape[dim] // shards_of).reshape((-1,) + (1,) * (len(shape) - dim - 1))

    factor_of = one(*split[0])
    for cut in split[1:]:
        factor_of = factor_of * one(*cut)
    return factor_of


def length_profile(amount, total, limit, lean):
    weights = [(1 << 20) // math.isqrt(grade ** lean) + 1 for grade in range(2, amount + 1)]
    spare, holding = total - limit - (amount - 1), [1] * (amount - 1)
    while spare > 0:
        free = [i for i in range(amount - 1) if holding[i] < limit]
        mass, budget = sum([weights[i] for i in free]), spare
        for i in free:
            extra = min(limit - holding[i], max(1, budget * weights[i] // mass), spare)
            holding[i] = holding[i] + extra
            spare = spare - extra
    return np.array([limit] + holding)


def ragged_sizes(key, number_of, total, bound, skew):
    if number_of == 2:
        one = jax.random.randint(key, (), max(1, total - bound), min(bound, total - 1) + 1)
        return jnp.stack([one, total - one])
    lengths = jnp.asarray(length_profile(number_of, total, bound, skew), jnp.int32)
    pairs = (number_of - 1) // 2
    giver, receiver = lengths[1:1 + 2 * pairs:2], lengths[2:2 + 2 * pairs:2]
    room = jnp.minimum(giver - 1, bound - receiver)
    moved = jax.random.randint(jax.random.fold_in(key, 1), (pairs,), 0, 1 << 20) % (room + 1)
    lengths = lengths.at[1:1 + 2 * pairs:2].set(giver - moved).at[2:2 + 2 * pairs:2].set(receiver + moved)
    return lengths[jax.random.permutation(jax.random.fold_in(key, 2), number_of)]


def deal_out(stream_key, own, number, rows, count, top, limit, slope):
    sequence = jax.random.permutation(stream_key, count)
    heavy_load, ordinary = portions_of(count, rows * top, limit, slope, True), portions_of(count, rows * top, limit, slope, False)
    places = jnp.arange(count)

    def named(sizes, rotation):
        used = int((sizes > 0).sum())
        fixed = max(1, used // 4)
        shifted = fixed + (places - fixed + rotation * (used - fixed)) % max(1, count - fixed)
        return jnp.zeros((count,), jnp.int32).at[sequence[jnp.where(places < fixed, places, shifted)]].set(jnp.asarray(sizes, jnp.int32))

    sizes = jnp.where(number % 4 == 0, named(heavy_load, number // 4), named(ordinary, number - number // 4 - 1))
    mixed = jax.random.permutation(jax.random.fold_in(own, 3), count)
    giver, receiver = mixed[0:count // 2 * 2:2], mixed[1:count // 2 * 2:2]
    room = jnp.minimum(sizes[giver] - 1, limit - sizes[receiver]) // 2
    room = jnp.where((giver == sequence[0]) | (receiver == sequence[0]) | (sizes[receiver] == 0), 0, jnp.maximum(room, 0))
    shifted = jax.random.randint(jax.random.fold_in(own, 4), (count // 2,), 0, 1 << 20) % (room + 1)
    sizes = sizes.at[giver].add(-shifted).at[receiver].add(shifted)
    labels = jnp.searchsorted(jnp.cumsum(sizes), jnp.arange(rows * top), side="right").astype(jnp.int32)
    listing = labels.reshape(top, rows).T
    listing = listing[jax.random.permutation(jax.random.fold_in(own, 1), rows)]
    rotation = jax.random.randint(jax.random.fold_in(own, 2), (rows, 1), 0, top)
    return jnp.take_along_axis(listing, (jnp.arange(top)[None, :] + rotation) % top, axis=1)


def portions_of(number_of, total, bound, slope, full):
    loads = [(1 << 20) // math.isqrt(rank ** slope) + 1 for rank in range(1, number_of + 1)]
    largest = bound if full else min(bound, max(-(-total // number_of), total * loads[0] // sum(loads)))
    least = 1 if total - largest >= number_of - 1 else 0
    holding, rest = [largest] + [least] * (number_of - 1), total - largest - least * (number_of - 1)
    while rest > 0:
        movable = [i for i in range(1, number_of) if holding[i] < largest] or [i for i in range(1, number_of) if holding[i] < bound]
        pool, budget = sum([loads[i] for i in movable]), rest
        for i in movable:
            extra = min(bound - holding[i], max(1, budget * loads[i] // pool), rest)
            holding[i] = holding[i] + extra
            rest = rest - extra
    return np.array(holding)


def noise(key, dims, scale, reach, split=(), kind=jnp.bfloat16):
    factor_of = steps_of(key, dims, split, -0.22, 0.18) if split else 1.0
    drawn = jax.random.normal(key, dims, jnp.float32) * scale * factor_of
    return jnp.minimum(jnp.maximum(drawn, -reach), reach).astype(kind)


def setup_inputs(seed: int = 0) -> dict:
    arg_keys = jax.random.split(jax.random.key(seed), 20)
    hidden = noise(arg_keys[0], (TOKENS, MODEL_WIDTH), 1.0, 6.0, ((0, 32), (1, 4)))
    segments = jax.vmap(lambda own: jnp.searchsorted(jnp.cumsum(ragged_sizes(own, REQS, TOK_COL, MAX_LEN, 2)), jnp.arange(TOK_COL), side="right"))(jax.random.split(arg_keys[1], COLUMNS)).reshape((COLUMNS, TOK_COL)).astype(jnp.int32)
    request_adapter = plant(jax.random.randint(arg_keys[2], (COLUMNS, REQS), 0, ADAPTER_COUNT), jax.random.fold_in(arg_keys[2], 1), 0, ADAPTER_COUNT - 1).astype(jnp.int32)
    routes_keys = jax.random.split(jax.random.fold_in(arg_keys[3], 1), COLUMNS * TOK_COL // TOK_DEV)
    routes_turns = jax.random.permutation(jax.random.fold_in(arg_keys[3], 3), COLUMNS * TOK_COL // TOK_DEV)
    routes = jax.vmap(lambda own, number: deal_out(jax.random.fold_in(arg_keys[3], 2), own, number, TOK_DEV, EXPERTS, TOP, CAP, 1))(routes_keys, routes_turns).reshape((COLUMNS, TOK_COL, TOP))
    expert_gates = jnp.clip(0.049804688 + 0.54785156 * jax.random.uniform(arg_keys[4], (COLUMNS, TOK_COL, TOP), jnp.float32) ** steps_of(arg_keys[4], (COLUMNS, TOK_COL, TOP), ((0, 32), (1, 4)), -0.2, 0.2), 0.049804688, 0.59765625).astype(jnp.bfloat16)
    attention_gain = jnp.clip(1.0 + 0.15 * jax.random.normal(arg_keys[5], (MODEL_WIDTH,), jnp.float32), 0.25, 1.75)
    joined_weight = noise(arg_keys[6], (MODEL_WIDTH, KEY_VALUE_HEADS, (QUERY_GROUP + 2) * HEAD_SIZE), MODEL_WIDTH ** -0.5, 0.109375, ((1, 4),))
    sinks = jnp.clip(3.0 * jax.random.uniform(arg_keys[7], (QUERY_HEADS,), jnp.float32) ** steps_of(arg_keys[7], (QUERY_HEADS,), ((0, 4),), -0.2, 0.2), 0.0, 3.0)
    attention_out_weight = noise(arg_keys[8], (QUERY_HEADS * HEAD_SIZE, MODEL_WIDTH), (QUERY_HEADS * HEAD_SIZE) ** -0.5, 0.125, ((0, 4),))
    joined_down_maps = noise(arg_keys[9], (MODEL_WIDTH, ADAPTER_COUNT * ADAPTER_RANK), MODEL_WIDTH ** -0.5, 0.109375)
    joined_up_maps = noise(arg_keys[10], (ADAPTER_COUNT * ADAPTER_RANK, KEY_VALUE_HEADS, (QUERY_GROUP + 2) * HEAD_SIZE), (16 * ADAPTER_RANK) ** -0.5, 0.375, ((1, 4),))
    output_down_maps = noise(arg_keys[11], (QUERY_HEADS * HEAD_SIZE, ADAPTER_COUNT * ADAPTER_RANK), (QUERY_HEADS * HEAD_SIZE) ** -0.5, 0.125, ((0, 4),))
    output_up_maps = noise(arg_keys[12], (ADAPTER_COUNT * ADAPTER_RANK, MODEL_WIDTH), (4 * ADAPTER_RANK) ** -0.5, 0.75, ((1, 4),))
    expert_norm_gain = jnp.clip(1.0 + 0.15 * jax.random.normal(arg_keys[13], (MODEL_WIDTH,), jnp.float32), 0.25, 1.75)
    expert_gate_weight = noise(arg_keys[14], (EXPERTS, MODEL_WIDTH, FF), MODEL_WIDTH ** -0.5, 0.109375, ((0, 32), (2, 4)))
    expert_up_weight = noise(arg_keys[15], (EXPERTS, MODEL_WIDTH, FF), MODEL_WIDTH ** -0.5, 0.109375, ((0, 32), (2, 4)))
    expert_down_weight = noise(arg_keys[16], (EXPERTS, FF, MODEL_WIDTH), FF ** -0.5, 0.109375, ((0, 32), (1, 4)))
    closing_gain = jnp.clip(1.0 + 0.15 * jax.random.normal(arg_keys[17], (MODEL_WIDTH,), jnp.float32), 0.25, 1.75)
    vocabulary_weight = noise(arg_keys[18], (MODEL_WIDTH, VOCAB), MODEL_WIDTH ** -0.5, 0.109375, ((1, 128),))
    return dict(hidden=hidden, segments=segments, request_adapter=request_adapter, routes=routes, expert_gates=expert_gates, attention_gain=attention_gain, joined_weight=joined_weight, sinks=sinks, attention_out_weight=attention_out_weight, joined_down_maps=joined_down_maps, joined_up_maps=joined_up_maps, output_down_maps=output_down_maps, output_up_maps=output_up_maps, expert_norm_gain=expert_norm_gain, expert_gate_weight=expert_gate_weight, expert_up_weight=expert_up_weight, expert_down_weight=expert_down_weight, closing_gain=closing_gain, vocabulary_weight=vocabulary_weight)


epsilon = 1e-05
theta_base = 150000.0
adapter_scale = 2.0
glu_alpha = 1.702

def rms_scale(values, gain_row):
    mean_square = lax.optimization_barrier(jnp.mean(values * values, axis=-1, keepdims=True))
    return values * lax.rsqrt(mean_square + epsilon) * gain_row

def positions_of(segment_row):
    counter = jnp.arange(segment_row.shape[0], dtype=jnp.int32)
    starting = jnp.concatenate([jnp.ones((1,), dtype=jnp.bool_), segment_row[1:] != segment_row[:-1]])
    first_index = lax.cummax(jnp.where(starting, counter, 0), axis=0)
    return counter - first_index

def adapter_per_token(segment_row, adapter_row):
    hits = segment_row[:, None] == jnp.arange(adapter_row.shape[0], dtype=jnp.int32)[None, :]
    return lax.optimization_barrier(jnp.sum(jnp.where(hits, adapter_row[None, :], 0), axis=1))

def rotate_heads(values, positions):
    head_dim = values.shape[-1]
    half_dim = head_dim // 2
    frequency = theta_base ** (-2.0 * jnp.arange(half_dim, dtype=jnp.float32) / head_dim)
    angles = positions.astype(jnp.float32)[:, None] * frequency[None, :]
    cosine = jnp.cos(angles)[:, None, :]
    sine_part = jnp.sin(angles)[:, None, :]
    first_half = values[..., :half_dim]
    second_half = values[..., half_dim:]
    return jnp.concatenate([first_half * cosine - second_half * sine_part, second_half * cosine + first_half * sine_part], axis=-1)

def attend_heads(queries, key_heads, value_heads, segment_row, sink_row):
    tokens_now, kv_now, group_now, head_dim = queries.shape
    scores = jnp.einsum('tkgh,skh->kgts', queries.astype(jnp.float32), key_heads.astype(jnp.float32)) * head_dim ** (-0.5)
    counter = jnp.arange(tokens_now, dtype=jnp.int32)
    allowed = (segment_row[:, None] == segment_row[None, :]) & (counter[None, :] <= counter[:, None])
    weights = jnp.where(allowed[None, None], jnp.exp(scores), 0.0)
    totals = lax.optimization_barrier(jnp.sum(weights, axis=-1, keepdims=True)) + jnp.exp(sink_row).reshape(kv_now, group_now, 1, 1)
    probs = lax.optimization_barrier((weights / totals).astype(jnp.bfloat16))
    blended_hidden = jnp.einsum('kgts,skh->tkgh', probs.astype(jnp.float32), value_heads.astype(jnp.float32))
    return blended_hidden.astype(jnp.bfloat16).reshape(tokens_now, kv_now * group_now * head_dim)

def reference(hidden, segments, request_adapter, routes, expert_gates, attention_gain, joined_weight, sinks, attention_out_weight, joined_down_maps, joined_up_maps, output_down_maps, output_up_maps, expert_norm_gain, expert_gate_weight, expert_up_weight, expert_down_weight, closing_gain, vocabulary_weight):
    reduced_every_adapter = ADAPTER_COUNT * ADAPTER_RANK
    rank_owner = jnp.arange(reduced_every_adapter, dtype=jnp.int32) // ADAPTER_RANK

    def column_layer(inputs):
        column_rows, segment_row, adapter_row = inputs
        normalized_hidden = rms_scale(column_rows.astype(jnp.float32), attention_gain).astype(jnp.bfloat16)
        joined_projection = jnp.dot(normalized_hidden, joined_weight.reshape(MODEL_WIDTH, -1), preferred_element_type=jnp.float32)
        reduced_hidden = jnp.dot(normalized_hidden, joined_down_maps, preferred_element_type=jnp.float32).astype(jnp.bfloat16)
        adapter_mask = adapter_per_token(segment_row, adapter_row)[:, None] == rank_owner[None, :]
        selected_reduced = jnp.where(adapter_mask, reduced_hidden, jnp.zeros_like(reduced_hidden))
        joined_projection = joined_projection + adapter_scale * jnp.dot(selected_reduced, joined_up_maps.reshape(reduced_every_adapter, -1), preferred_element_type=jnp.float32)
        joined_projection = joined_projection.reshape(TOK_COL, KEY_VALUE_HEADS, QUERY_GROUP + 2, HEAD_SIZE)
        positions = positions_of(segment_row)
        queries = rotate_heads(joined_projection[:, :, :QUERY_GROUP].reshape(TOK_COL, KEY_VALUE_HEADS * QUERY_GROUP, HEAD_SIZE), positions)
        queries = lax.optimization_barrier(queries.astype(jnp.bfloat16)).reshape(TOK_COL, KEY_VALUE_HEADS, QUERY_GROUP, HEAD_SIZE)
        key_heads = lax.optimization_barrier(rotate_heads(joined_projection[:, :, QUERY_GROUP], positions).astype(jnp.bfloat16))
        value_heads = lax.optimization_barrier(joined_projection[:, :, QUERY_GROUP + 1].astype(jnp.bfloat16))
        blended_hidden = attend_heads(queries, key_heads, value_heads, segment_row, sinks)
        attention_output = jnp.dot(blended_hidden, attention_out_weight, preferred_element_type=jnp.float32)
        output_reduced = jnp.dot(blended_hidden, output_down_maps, preferred_element_type=jnp.float32).astype(jnp.bfloat16)
        selected_output = jnp.where(adapter_mask, output_reduced, jnp.zeros_like(output_reduced))
        attention_output = attention_output + adapter_scale * jnp.dot(selected_output, output_up_maps, preferred_element_type=jnp.float32)
        return (column_rows.astype(jnp.float32) + attention_output).astype(jnp.bfloat16)
    resid = lax.map(column_layer, (hidden.reshape(COLUMNS, TOK_COL, MODEL_WIDTH), segments, request_adapter)).reshape(TOKENS, MODEL_WIDTH)
    resid = lax.optimization_barrier(resid)
    moe_in = rms_scale(resid.astype(jnp.float32), expert_norm_gain).astype(jnp.bfloat16)
    blocks = TOKENS // TOK_DEV
    route_rows = routes.reshape(blocks, TOK_DEV * TOP)
    gate_rows = expert_gates.reshape(blocks, TOK_DEV * TOP).astype(jnp.float32)
    one_hot = (route_rows[:, :, None] == jnp.arange(EXPERTS, dtype=jnp.int32)[None, None, :]).astype(jnp.int32)
    slot_rows = lax.optimization_barrier(jnp.sum((jnp.cumsum(one_hot, axis=1) - one_hot) * one_hot, axis=2))
    block_ids = jnp.broadcast_to(jnp.arange(blocks, dtype=jnp.int32)[:, None], route_rows.shape)
    token_ids = block_ids * TOK_DEV + jnp.arange(TOK_DEV * TOP, dtype=jnp.int32)[None, :] // TOP
    table = jnp.full((EXPERTS, blocks, CAP), TOKENS, jnp.int32).at[route_rows, block_ids, slot_rows].set(token_ids)
    gate_table = jnp.zeros((EXPERTS, blocks, CAP), jnp.float32).at[route_rows, block_ids, slot_rows].set(gate_rows)
    padded = jnp.concatenate([moe_in, jnp.zeros((1, MODEL_WIDTH), jnp.bfloat16)], axis=0)
    quarter_units = FF // N_DP

    def one_expert(running, inputs):
        gate_weight, up_weight, down_weight, rows_index, row_gates = inputs
        flat_index = rows_index.reshape(-1).astype(jnp.int32)
        rows_in = jnp.take(padded, flat_index, axis=0)
        gate_part = jnp.dot(rows_in, gate_weight, preferred_element_type=jnp.float32)
        up_part = jnp.dot(rows_in, up_weight, preferred_element_type=jnp.float32)
        activated = (gate_part * jax.nn.sigmoid(glu_alpha * gate_part) * (up_part + 1.0)).astype(jnp.bfloat16)
        summed = jnp.zeros((flat_index.shape[0], MODEL_WIDTH), jnp.float32)
        for quarter in range(N_DP):
            first_unit = quarter * quarter_units
            piece_out = jnp.dot(activated[:, first_unit:first_unit + quarter_units], down_weight[first_unit:first_unit + quarter_units], preferred_element_type=jnp.float32)
            summed = summed + lax.optimization_barrier(piece_out.astype(jnp.bfloat16)).astype(jnp.float32)
        expert_out = lax.optimization_barrier(summed.astype(jnp.bfloat16)).astype(jnp.float32)
        running = running.at[flat_index].add(row_gates.reshape(-1, 1) * expert_out)
        return (running, None)
    moe_sum, unused = lax.scan(one_expert, jnp.zeros((TOKENS + 1, MODEL_WIDTH), jnp.float32), (expert_gate_weight, expert_up_weight, expert_down_weight, table, gate_table))
    moe = lax.optimization_barrier(moe_sum[:TOKENS].astype(jnp.bfloat16))
    hidden_out = (resid.astype(jnp.float32) + moe.astype(jnp.float32)).astype(jnp.bfloat16)
    column_out = lax.optimization_barrier(hidden_out).reshape(COLUMNS, TOK_COL, MODEL_WIDTH)
    counter = jnp.arange(TOK_COL, dtype=jnp.int32)
    request_ids = jnp.arange(REQS, dtype=jnp.int32)
    last_index = lax.optimization_barrier(jnp.max(jnp.where(segments[:, None, :] == request_ids[None, :, None], counter[None, None, :], -1), axis=2))
    end_rows = jax.vmap(lambda rows, where_at: jnp.take(rows, where_at, axis=0))(column_out, last_index)
    ends = rms_scale(end_rows.astype(jnp.float32), closing_gain).astype(jnp.bfloat16).reshape(LAST, MODEL_WIDTH)
    logits = jnp.dot(ends, vocabulary_weight, preferred_element_type=jnp.float32)
    return (hidden_out, logits)
```

```python
import functools

import jax
import jax.numpy as jnp
from jax import lax
from jax.experimental import pallas as pl
from jax.experimental.pallas import tpu as pltpu
from jax.sharding import PartitionSpec as P

HEAD_SIZE = 64
QUERY_GROUP = 8
TOP = 4
ADAPTER_RANK = 16
REQS = 4
CAP = 16
CHUNKS = 4

epsilon = 1e-05
theta_base = 150000.0
adapter_scale = 2.0
glu_alpha = 1.702

MESH = pl.DeviceIdType.MESH
BF = jnp.bfloat16
F32 = jnp.float32
VMEM = pl.BlockSpec(memory_space=pltpu.VMEM)
ANY = pl.BlockSpec(memory_space=pl.ANY)


def dot(a, b):
    return jnp.dot(a, b, preferred_element_type=F32)


def place():
    z, n = lax.axis_index("dp"), lax.axis_size("dp")
    c, m = lax.axis_index("expert"), lax.axis_size("expert")
    return z, n, c, m


def greet_z(offsets):
    z, n, c, _ = place()
    barrier = pltpu.get_barrier_semaphore()
    for o in offsets:
        pl.semaphore_signal(barrier, inc=1, device_id=(lax.rem(z + o, n), c), device_id_type=MESH)
    pl.semaphore_wait(barrier, len(offsets))


def send(src, dst, send_sem, recv_sem, device):
    copy = pltpu.make_async_remote_copy(
        src_ref=src, dst_ref=dst, send_sem=send_sem, recv_sem=recv_sem, device_id=device, device_id_type=MESH
    )
    copy.start()
    return copy


def wait_bytes(ref, sem):
    pltpu.make_async_copy(ref, ref, sem).wait()


def gather_kernel(x_ref, a_ref, xo_ref, ao_ref, ss, rs, local):
    z, n, c, _ = place()
    greet_z((1, 2, 3))
    own = pltpu.make_async_copy(x_ref, xo_ref.at[z], local.at[0])
    own.start()
    own_a = pltpu.make_async_copy(a_ref, ao_ref.at[z], local.at[1])
    own_a.start()
    half = x_ref.shape[0] // 2
    zu, zd = lax.rem(z + 1, n), lax.rem(z + 3, n)
    up, down, far = (zu, c), (zd, c), (lax.rem(z + 2, n), c)
    lo, hi = pl.ds(0, half), pl.ds(half, half)
    copies = [
        send(x_ref.at[lo], xo_ref.at[z, lo], ss.at[0], rs.at[0], up),
        send(x_ref.at[hi], xo_ref.at[z, hi], ss.at[1], rs.at[1], down),
        send(a_ref, ao_ref.at[z], ss.at[6], rs.at[6], up),
        send(a_ref, ao_ref.at[z], ss.at[7], rs.at[7], down),
        send(a_ref, ao_ref.at[z], ss.at[8], rs.at[8], far),
        send(x_ref.at[hi], xo_ref.at[z, hi], ss.at[2], rs.at[2], up),
        send(x_ref.at[lo], xo_ref.at[z, lo], ss.at[3], rs.at[3], down),
    ]
    copies[0].wait_recv()
    copies.append(send(xo_ref.at[zd, lo], xo_ref.at[zd, lo], ss.at[4], rs.at[4], up))
    copies[1].wait_recv()
    copies.append(send(xo_ref.at[zu, hi], xo_ref.at[zu, hi], ss.at[5], rs.at[5], down))
    for copy in copies[2:]:
        copy.wait_recv()
    for copy in copies:
        copy.wait_send()
    own.wait()
    own_a.wait()


def gather_z(hidden, aux):
    n = lax.axis_size("dp")
    return pl.pallas_call(
        gather_kernel,
        out_shape=(
            jax.ShapeDtypeStruct((n,) + hidden.shape, hidden.dtype),
            jax.ShapeDtypeStruct((n,) + aux.shape, aux.dtype),
        ),
        in_specs=[VMEM, VMEM],
        out_specs=(VMEM, VMEM),
        scratch_shapes=[
            pltpu.SemaphoreType.DMA((9,)),
            pltpu.SemaphoreType.DMA((9,)),
            pltpu.SemaphoreType.DMA((2,)),
        ],
        compiler_params=pltpu.CompilerParams(
            collective_id=0, has_side_effects=True, vmem_limit_bytes=32 * 2**20
        ),
    )(hidden, aux)


def out_kernel(
    b_ref, wo_ref, odm_ref, hid_ref, mask_ref, oum_ref, gain_ref,
    resid_ref, moe_ref,
    low_snd, low_rcv, snd, rcv, st_snd, st_rcv, ss, rs,
):
    z, n, c, _ = place()
    blended = b_ref[...]
    low = dot(blended, odm_ref[...]).astype(BF)
    low_snd[...] = low
    greet_z((1, 2, 3))
    copies = []
    for o in (2, 1, 3):
        peer = (lax.rem(z + o, n), c)
        copies.append(send(low_snd, low_rcv.at[o - 1], ss.at[o - 1], rs.at[o - 1], peer))
    for o in (2, 1, 3):
        q = lax.rem(z + o, n)
        snd[o - 1] = dot(blended, wo_ref[q]).astype(BF)
        copies.append(send(snd.at[o - 1], rcv.at[o - 1], ss.at[o + 2], rs.at[o + 2], (q, c)))
    total = hid_ref[...].astype(F32) + dot(blended, wo_ref[z]).astype(BF).astype(F32)
    for copy in copies[:3]:
        copy.wait_recv()
    low_sum = low.astype(F32)
    for k in range(3):
        low_sum = low_sum + low_rcv[k].astype(F32)
    picked = (low_sum * mask_ref[...]).astype(BF)
    total = total + adapter_scale * dot(picked, oum_ref[...])
    for copy in copies[3:]:
        copy.wait_recv()
    for k in range(3):
        total = total + rcv[k].astype(F32)
    resid = total.astype(BF)
    resid_ref[...] = resid
    wide = resid.astype(F32)
    sums = jnp.sum(wide * wide, axis=1, keepdims=True)
    st_snd[...] = jnp.broadcast_to(sums, (sums.shape[0], 128)).T[:8]
    more = []
    for o in (2, 1, 3):
        more.append(send(st_snd, st_rcv.at[o - 1], ss.at[o + 5], rs.at[o + 5], (lax.rem(z + o, n), c)))
    for copy in more:
        copy.wait_recv()
    every = st_snd[...] + st_rcv[0] + st_rcv[1] + st_rcv[2]
    width = hid_ref.shape[1] * 4
    scale = lax.rsqrt(every / width + epsilon)
    column = jnp.concatenate([scale] * 16, axis=0).T[:, :1]
    moe_ref[...] = (wide * column * gain_ref[...]).astype(BF)
    for copy in copies + more:
        copy.wait_send()


def out_project(blended, wo4, odm, hidden, mask, oum, gain):
    rows, q = hidden.shape
    n = 3
    return pl.pallas_call(
        out_kernel,
        out_shape=(jax.ShapeDtypeStruct((rows, q), BF), jax.ShapeDtypeStruct((rows, q), BF)),
        in_specs=[VMEM] * 7,
        out_specs=(VMEM, VMEM),
        scratch_shapes=[
            pltpu.VMEM(mask.shape, BF),
            pltpu.VMEM((n,) + mask.shape, BF),
            pltpu.VMEM((n, rows, q), BF),
            pltpu.VMEM((n, rows, q), BF),
            pltpu.VMEM((8, rows), F32),
            pltpu.VMEM((n, 8, rows), F32),
            pltpu.SemaphoreType.DMA((9,)),
            pltpu.SemaphoreType.DMA((9,)),
        ],
        compiler_params=pltpu.CompilerParams(
            collective_id=1, has_side_effects=True, vmem_limit_bytes=48 * 2**20
        ),
    )(blended, wo4, odm, hidden, mask, oum, gain)


def expert_kernel(
    slots, d_ref, mi_ref, wg_hbm, wu_hbm, wd_hbm, out_hbm,
    mi_nb, stg, xb, wg, wu, wd, yo, ys, yr,
    w_sem, mi_sem, ds, dr, zs, zr, ps, pr, bs, br, own_sem,
):
    z, n, c, m = place()
    up, down = lax.rem(z + 1, n), lax.rem(z + 3, n)
    rows = slots * m
    per = m // CHUNKS
    span = per * slots
    q = mi_ref.shape[1]
    quarters = (z, down, up, lax.rem(z + 2, n))
    weights = []
    for r in range(4):
        at = pl.ds(pl.multiple_of(quarters[r] * q, 16), q)
        weights.append(pltpu.make_async_copy(wg_hbm.at[at], wg.at[r], w_sem.at[0, r]))
        weights.append(pltpu.make_async_copy(wu_hbm.at[at], wu.at[r], w_sem.at[1, r]))
        weights.append(pltpu.make_async_copy(wd_hbm.at[quarters[r]], wd.at[r], w_sem.at[2, r]))
    for w in weights:
        w.start()
    barrier = pltpu.get_barrier_semaphore()

    @pl.loop(1, m)
    def _(j):
        pl.semaphore_signal(barrier, inc=1, device_id=(z, lax.rem(c + j, m)), device_id_type=MESH)

    for peer in (up, down):
        pl.semaphore_signal(barrier, inc=1, device_id=(peer, c), device_id_type=MESH)
    pl.semaphore_wait(barrier, m + 1)
    first = send(mi_ref, mi_nb, mi_sem.at[0], mi_sem.at[1], (up, c))

    def chunk(ch):
        return pl.ds(ch * span, span)

    def dispatch(ch, r):
        source = mi_ref if r == 0 else mi_nb
        stg[r, chunk(ch)] = dot(d_ref[chunk(ch)], source[...]).astype(BF)

        @pl.loop(max(1, ch * per), (ch + 1) * per)
        def _(j):
            at = pl.ds(pl.multiple_of(j * slots, slots), slots)
            send(stg.at[r, at], xb.at[r, at], ds.at[r, ch], dr.at[r, ch], (z, lax.rem(c + j, m)))

        if ch == 0:
            xb[r, :slots] = stg[r, :slots]

    def but_own(ch):
        return pl.ds(slots, span - slots) if ch == 0 else chunk(ch)

    def forward(ch):
        wait_bytes(xb.at[0, but_own(ch)], dr.at[0, ch])
        send(xb.at[0, chunk(ch)], xb.at[2, chunk(ch)], zs.at[0, ch], zr.at[0, ch], (down, c))
        wait_bytes(xb.at[1, but_own(ch)], dr.at[1, ch])
        send(xb.at[1, chunk(ch)], xb.at[3, chunk(ch)], zs.at[1, ch], zr.at[1, ch], (up, c))

    tile = min(256, span)

    def experts(ch):
        wait_bytes(xb.at[2, chunk(ch)], zr.at[0, ch])
        wait_bytes(xb.at[3, chunk(ch)], zr.at[1, ch])

        @pl.loop(0, span // tile)
        def _(t):
            at = pl.ds(pl.multiple_of(ch * span + t * tile, tile), tile)
            gate = dot(xb[0, at], wg[0])
            for r in range(1, 4):
                gate = gate + dot(xb[r, at], wg[r])
            lift = dot(xb[0, at], wu[0])
            for r in range(1, 4):
                lift = lift + dot(xb[r, at], wu[r])
            act = (gate * jax.nn.sigmoid(glu_alpha * gate) * (lift + 1.0)).astype(BF)
            for r in range(2, 4):
                ys[r - 2, at] = dot(act, wd[r]).astype(BF)
            for r in range(2):
                yo[r, at] = dot(act, wd[r]).astype(BF)

        send(ys.at[0, chunk(ch)], yr.at[0, chunk(ch)], ps.at[0, ch], pr.at[0, ch], (up, c))
        send(ys.at[1, chunk(ch)], yr.at[1, chunk(ch)], ps.at[1, ch], pr.at[1, ch], (down, c))

    def give_back(ch):
        for r in range(2):
            wait_bytes(yr.at[r, chunk(ch)], pr.at[r, ch])
            yo[r, chunk(ch)] = (yo[r, chunk(ch)].astype(F32) + yr[r, chunk(ch)].astype(F32)).astype(BF)

            @pl.loop(max(1, ch * per), (ch + 1) * per)
            def _(j):
                at = pl.ds(pl.multiple_of(j * slots, slots), slots)
                send(yo.at[r, at], out_hbm.at[r, at], bs.at[r, ch], br.at[r, ch], (z, lax.rem(c + m - j, m)))

            if ch == 0:
                pltpu.make_async_copy(yo.at[r, pl.ds(0, slots)], out_hbm.at[r, pl.ds(0, slots)], own_sem.at[r]).start()

    dispatch(0, 0)
    dispatch(1, 0)
    first.wait_recv()
    dispatch(0, 1)
    dispatch(1, 1)
    for ch in range(2, CHUNKS):
        dispatch(ch, 0)
        dispatch(ch, 1)
    forward(0)
    for w in weights:
        w.wait()
    for ch in range(CHUNKS):
        if ch + 1 < CHUNKS:
            forward(ch + 1)
        experts(ch)
        if ch:
            give_back(ch - 1)
    give_back(CHUNKS - 1)
    first.wait_send()
    for r in range(2):
        for ch in range(CHUNKS):
            wait_bytes(stg.at[r, but_own(ch)], ds.at[r, ch])
            wait_bytes(xb.at[r, chunk(ch)], zs.at[r, ch])
            wait_bytes(ys.at[r, chunk(ch)], ps.at[r, ch])
            wait_bytes(yo.at[r, but_own(ch)], bs.at[r, ch])
            wait_bytes(out_hbm.at[r, but_own(ch)], br.at[r, ch])
        wait_bytes(out_hbm.at[r, pl.ds(0, slots)], own_sem.at[r])


def experts_call(pick, moe_in, wg, wu, wd4, slots):
    rows, q = pick.shape[0], moe_in.shape[1]
    f = wg.shape[1]
    dma = lambda *s: pltpu.SemaphoreType.DMA(s)
    big = lambda k: pltpu.VMEM((k, rows, q), BF)
    return pl.pallas_call(
        functools.partial(expert_kernel, slots),
        out_shape=jax.ShapeDtypeStruct((2, rows, q), BF),
        in_specs=[VMEM, VMEM, ANY, ANY, ANY],
        out_specs=ANY,
        scratch_shapes=[
            pltpu.VMEM(moe_in.shape, BF),
            big(2), big(4),
            pltpu.VMEM((4, q, f), BF), pltpu.VMEM((4, q, f), BF), pltpu.VMEM((4, f, q), BF),
            big(2), big(2), big(2),
            dma(3, 4), dma(2),
            dma(2, CHUNKS), dma(2, CHUNKS), dma(2, CHUNKS), dma(2, CHUNKS),
            dma(2, CHUNKS), dma(2, CHUNKS), dma(2, CHUNKS), dma(2, CHUNKS), dma(2),
        ],
        compiler_params=pltpu.CompilerParams(
            collective_id=2, has_side_effects=True, vmem_limit_bytes=62 * 2**20
        ),
    )(pick, moe_in, wg, wu, wd4)


def finish_kernel(m0_ref, m1_ref, resid_ref, out_ref, rcv, sem):
    z, n, c, _ = place()
    up, down = lax.rem(z + 1, n), lax.rem(z + 3, n)
    greet_z((1, 3))
    copy = send(m1_ref, rcv, sem.at[0], sem.at[1], (down, c))
    copy.wait_recv()
    moe = (m0_ref[...] + rcv[...].astype(F32)).astype(BF)
    out_ref[...] = (resid_ref[...].astype(F32) + moe.astype(F32)).astype(BF)
    copy.wait_send()


def finish(m0, m1, resid):
    return pl.pallas_call(
        finish_kernel,
        out_shape=jax.ShapeDtypeStruct(resid.shape, BF),
        in_specs=[VMEM] * 3,
        out_specs=VMEM,
        scratch_shapes=[pltpu.VMEM(resid.shape, BF), pltpu.SemaphoreType.DMA((2,))],
        compiler_params=pltpu.CompilerParams(
            collective_id=3, has_side_effects=True, vmem_limit_bytes=32 * 2**20
        ),
    )(m0, m1, resid)


def rms_scale(values, gain_row):
    mean_square = jnp.mean(values * values, axis=-1, keepdims=True)
    return values * lax.rsqrt(mean_square + epsilon) * gain_row


def rotate(values, cosine, sine):
    half = values.shape[-1] // 2
    first, second = values[..., :half], values[..., half:]
    return jnp.concatenate([first * cosine - second * sine, second * cosine + first * sine], axis=-1)


def attend_heads(queries, keys, values, segment_row, sink_row):
    tokens, group, head_dim = queries.shape
    scores = jnp.einsum("tgh,sh->gts", queries, keys, preferred_element_type=F32) * head_dim ** (-0.5)
    counter = jnp.arange(tokens, dtype=jnp.int32)
    allowed = (segment_row[:, None] == segment_row[None, :]) & (counter[None, :] <= counter[:, None])
    weights = jnp.where(allowed[None], jnp.exp(scores), 0.0)
    totals = jnp.sum(weights, axis=-1, keepdims=True) + jnp.exp(sink_row).reshape(group, 1, 1)
    probs = (weights / totals).astype(BF)
    blended = jnp.einsum("gts,sh->tgh", probs, values, preferred_element_type=F32)
    return blended.astype(BF).reshape(tokens, group * head_dim)


def shards(
    hidden, segments, request_adapter, routes, expert_gates, attention_gain, joined_weight, sinks,
    attention_out_weight, joined_down_maps, joined_up_maps, output_down_maps, output_up_maps,
    expert_norm_gain, expert_gate_weight, expert_up_weight, expert_down_weight, closing_gain, vocabulary_weight,
):
    groups, columns = lax.axis_size("dp"), lax.axis_size("expert")
    z, c = lax.axis_index("dp"), lax.axis_index("expert")
    segment_row, adapter_row = segments[0], request_adapter[0]
    tokens, quarter = hidden.shape
    width = quarter * groups
    share = tokens // groups
    aux = jnp.concatenate(
        [routes[0].astype(BF), expert_gates[0], jnp.zeros((share, 128 - 2 * TOP), BF)], axis=1
    )
    hid4, aux4 = gather_z(hidden, aux)
    rows = jnp.transpose(hid4, (1, 0, 2)).reshape(tokens, width)

    normed = rms_scale(rows.astype(F32), attention_gain).astype(BF)
    ranks = joined_down_maps.shape[1]
    projected = dot(normed, joined_weight.reshape(width, -1))
    low = dot(normed, joined_down_maps).astype(BF)
    request_ids = jnp.arange(REQS, dtype=jnp.int32)
    hits = segment_row[:, None] == request_ids[None, :]
    adapter = jnp.sum(jnp.where(hits, adapter_row[None, :], 0), axis=1)
    mask = adapter[:, None] == (jnp.arange(ranks, dtype=jnp.int32) // ADAPTER_RANK)[None, :]
    low = jnp.where(mask, low, jnp.zeros_like(low))
    projected = projected + adapter_scale * dot(low, joined_up_maps.reshape(ranks, -1))
    counter = jnp.arange(tokens, dtype=jnp.int32)
    starts = jnp.min(jnp.where(hits, counter[:, None], tokens), axis=0)
    positions = counter - jnp.sum(jnp.where(hits, starts[None, :], 0), axis=1)
    half = HEAD_SIZE // 2
    frequency = theta_base ** (-2.0 * jnp.arange(half, dtype=F32) / HEAD_SIZE)
    angles = positions.astype(F32)[:, None] * frequency[None, :]
    cosine, sine = jnp.cos(angles)[:, None, :], jnp.sin(angles)[:, None, :]
    projected = projected.reshape(tokens, QUERY_GROUP + 2, HEAD_SIZE)
    turned = rotate(projected[:, : QUERY_GROUP + 1], cosine, sine).astype(BF)
    blended = attend_heads(
        turned[:, :QUERY_GROUP], turned[:, QUERY_GROUP], projected[:, QUERY_GROUP + 1].astype(BF), segment_row, sinks
    )

    wo4 = jnp.transpose(attention_out_weight.reshape(-1, groups, quarter), (1, 0, 2))
    gain = lax.dynamic_slice_in_dim(expert_norm_gain, z * quarter, quarter)[None, :]
    resid, moe_in = out_project(
        blended, wo4, output_down_maps, hidden, mask.astype(F32), output_up_maps, gain
    )

    route_all = aux4[:, :, :TOP].reshape(tokens, TOP)
    gate_all = aux4[:, :, TOP : 2 * TOP].reshape(tokens, TOP)
    slots = CAP * groups
    targets = lax.rem(c + jnp.arange(columns, dtype=jnp.int32), columns).astype(BF)
    named = route_all[:, :, None] == targets[None, None, :]
    hit = jnp.any(named, axis=1)
    gate_of = jnp.sum(jnp.where(named, gate_all.astype(F32)[:, :, None], 0.0), axis=1)
    before = (counter[None, :] < counter[:, None]).astype(BF)
    rank = jnp.where(hit, dot(before, hit.astype(BF)), -1.0)
    slot_ids = jnp.arange(slots, dtype=F32)
    pick = (rank.T[:, None, :] == slot_ids[None, :, None]).astype(BF).reshape(columns * slots, tokens)
    weigh = jnp.where(rank[:, :, None] == slot_ids[None, None, :], gate_of[:, :, None], 0.0)
    weigh = weigh.astype(BF).reshape(tokens, columns * slots)

    wd4 = jnp.transpose(expert_down_weight[0].reshape(-1, groups, quarter), (1, 0, 2))
    answers = experts_call(pick, moe_in, expert_gate_weight[0], expert_up_weight[0], wd4, slots)
    m0 = dot(weigh, answers[0])
    m1 = dot(weigh, answers[1]).astype(BF)
    hidden_out = finish(m0, m1, resid)

    last = jnp.max(jnp.where(hits, counter[:, None], -1), axis=0)
    chosen = jnp.take(hidden_out, last, axis=0)
    spread = lax.all_gather(chosen, ("dp", "expert"), axis=0, tiled=True)
    ends = jnp.transpose(spread.reshape(groups, columns * REQS, quarter), (1, 0, 2)).reshape(-1, width)
    ends = rms_scale(ends.astype(F32), closing_gain).astype(BF)
    logits = dot(ends, vocabulary_weight)
    return hidden_out, logits


def solution(mesh):
    in_specs = (
        P("expert", "dp"),
        P("expert", None),
        P("expert", None),
        P("expert", "dp", None),
        P("expert", "dp", None),
        P(),
        P(None, "dp", None),
        P("dp"),
        P("dp", None),
        P(),
        P(None, "dp", None),
        P("dp", None),
        P(None, "dp"),
        P(),
        P("expert", None, "dp"),
        P("expert", None, "dp"),
        P("expert", "dp", None),
        P(),
        P(None, ("dp", "expert")),
    )
    out_specs = (P("expert", "dp"), P(None, ("dp", "expert")))
    return jax.shard_map(shards, mesh=mesh, in_specs=in_specs, out_specs=out_specs, check_vma=False)
```

```python
import functools

import jax
import jax.numpy as jnp
from jax import lax
from jax.experimental import pallas as pl
from jax.experimental.pallas import tpu as pltpu
from jax.sharding import PartitionSpec as P

HEAD_SIZE = 64
QUERY_GROUP = 8
TOP = 4
ADAPTER_RANK = 16
REQS = 4
CAP = 16
CHUNKS = 8
PER = 4
EARLY = 4
AHEAD = 2
BACK = 1
ABSORB = 2
SENDING = 5
RING = 3

epsilon = 1e-05
theta_base = 150000.0
adapter_scale = 2.0
glu_alpha = 1.702

MESH = pl.DeviceIdType.MESH
BF = jnp.bfloat16
F32 = jnp.float32
VMEM = pl.BlockSpec(memory_space=pltpu.VMEM)
ANY = pl.BlockSpec(memory_space=pl.ANY)


def dot(a, b):
    return jnp.dot(a, b, preferred_element_type=F32)


def dot_nt(a, b):
    return lax.dot_general(a, b, (((1,), (1,)), ((), ())), preferred_element_type=F32)


def dot_tn(a, b):
    return lax.dot_general(a, b, (((0,), (0,)), ((), ())), preferred_element_type=F32)


def place():
    z, n = lax.axis_index("dp"), lax.axis_size("dp")
    c, m = lax.axis_index("expert"), lax.axis_size("expert")
    return z, n, c, m


def greet_z(offsets):
    z, n, c, _ = place()
    barrier = pltpu.get_barrier_semaphore()
    for o in offsets:
        pl.semaphore_signal(barrier, inc=1, device_id=(lax.rem(z + o, n), c), device_id_type=MESH)
    pl.semaphore_wait(barrier, len(offsets))


def send(src, dst, send_sem, recv_sem, device):
    copy = pltpu.make_async_remote_copy(
        src_ref=src, dst_ref=dst, send_sem=send_sem, recv_sem=recv_sem, device_id=device, device_id_type=MESH
    )
    copy.start()
    return copy


def wait_bytes(ref, sem):
    pltpu.make_async_copy(ref, ref, sem).wait()


def gather_kernel(x_ref, a_ref, xo_ref, ao_ref, ss, rs, local):
    z, n, c, _ = place()
    greet_z((1, 2, 3))
    own = pltpu.make_async_copy(x_ref, xo_ref.at[z], local.at[0])
    own.start()
    own_a = pltpu.make_async_copy(a_ref, ao_ref.at[z], local.at[1])
    own_a.start()
    half = x_ref.shape[0] // 32 * 16
    zu, zd = lax.rem(z + 1, n), lax.rem(z + 3, n)
    up, down, far = (zu, c), (zd, c), (lax.rem(z + 2, n), c)
    lo, hi = pl.ds(0, half), pl.ds(half, x_ref.shape[0] - half)
    copies = [
        send(x_ref.at[lo], xo_ref.at[z, lo], ss.at[0], rs.at[0], up),
        send(x_ref.at[hi], xo_ref.at[z, hi], ss.at[1], rs.at[1], down),
        send(a_ref, ao_ref.at[z], ss.at[6], rs.at[6], up),
        send(a_ref, ao_ref.at[z], ss.at[7], rs.at[7], down),
        send(a_ref, ao_ref.at[z], ss.at[8], rs.at[8], far),
        send(x_ref.at[hi], xo_ref.at[z, hi], ss.at[2], rs.at[2], up),
        send(x_ref.at[lo], xo_ref.at[z, lo], ss.at[3], rs.at[3], down),
    ]
    copies[0].wait_recv()
    copies.append(send(xo_ref.at[zd, lo], xo_ref.at[zd, lo], ss.at[4], rs.at[4], up))
    copies[1].wait_recv()
    copies.append(send(xo_ref.at[zu, hi], xo_ref.at[zu, hi], ss.at[5], rs.at[5], down))
    for copy in copies[2:]:
        copy.wait_recv()
    for copy in copies:
        copy.wait_send()
    own.wait()
    own_a.wait()


def gather_z(hidden, aux):
    n = lax.axis_size("dp")
    return pl.pallas_call(
        gather_kernel,
        out_shape=(
            jax.ShapeDtypeStruct((n,) + hidden.shape, hidden.dtype),
            jax.ShapeDtypeStruct((n,) + aux.shape, aux.dtype),
        ),
        in_specs=[VMEM, VMEM],
        out_specs=(VMEM, VMEM),
        scratch_shapes=[
            pltpu.SemaphoreType.DMA((9,)),
            pltpu.SemaphoreType.DMA((9,)),
            pltpu.SemaphoreType.DMA((2,)),
        ],
        compiler_params=pltpu.CompilerParams(
            collective_id=0, has_side_effects=True, vmem_limit_bytes=32 * 2**20
        ),
    )(hidden, aux)


def out_kernel(
    b_ref, wo_ref, odm_ref, hid_ref, mask_ref, oum_ref, gain_ref,
    resid_ref, moe_ref,
    low_snd, low_rcv, snd, rcv, st_snd, st_rcv, ss, rs,
):
    z, n, c, _ = place()
    quarter = hid_ref.shape[0]
    blended = b_ref[...]

    def part(q):
        return dot(wo_ref[pl.ds(pl.multiple_of(q * quarter, 16), quarter)], blended).astype(BF)

    low = dot_tn(odm_ref[...], blended).astype(BF)
    low_snd[...] = low
    greet_z((1, 2, 3))
    copies = []
    for o in (2, 1, 3):
        q = lax.rem(z + o, n)
        snd[o - 1] = part(q)
        copies.append(send(snd.at[o - 1], rcv.at[o - 1], ss.at[o + 2], rs.at[o + 2], (q, c)))
        copies.append(send(low_snd, low_rcv.at[o - 1], ss.at[o - 1], rs.at[o - 1], (q, c)))
    total = hid_ref[...].astype(F32) + part(z).astype(F32)
    for copy in copies[1::2]:
        copy.wait_recv()
    low_sum = low.astype(F32)
    for k in range(3):
        low_sum = low_sum + low_rcv[k].astype(F32)
    picked = (low_sum * mask_ref[...]).astype(BF)
    total = total + adapter_scale * dot(oum_ref[...], picked)
    for copy in copies[0::2]:
        copy.wait_recv()
    for k in range(3):
        total = total + rcv[k].astype(F32)
    resid = total.astype(BF)
    resid_ref[...] = resid
    wide = resid.astype(F32)
    sums = jnp.sum(wide * wide, axis=0, keepdims=True)
    st_snd[...] = jnp.broadcast_to(sums, st_snd.shape)
    more = []
    for o in (2, 1, 3):
        more.append(send(st_snd, st_rcv.at[o - 1], ss.at[o + 5], rs.at[o + 5], (lax.rem(z + o, n), c)))
    for copy in more:
        copy.wait_recv()
    every = st_snd[...] + st_rcv[0] + st_rcv[1] + st_rcv[2]
    scale = lax.rsqrt(every / (4.0 * quarter) + epsilon)
    moe_ref[...] = (wide * scale[:1] * gain_ref[...]).astype(BF)
    for copy in copies + more:
        copy.wait_send()


def out_project(blended, wo, odm, hidden, mask, oum, gain):
    q, rows = hidden.shape
    n = 3
    return pl.pallas_call(
        out_kernel,
        out_shape=(jax.ShapeDtypeStruct((q, rows), BF), jax.ShapeDtypeStruct((q, rows), BF)),
        in_specs=[VMEM] * 7,
        out_specs=(VMEM, VMEM),
        scratch_shapes=[
            pltpu.VMEM(mask.shape, BF),
            pltpu.VMEM((n,) + mask.shape, BF),
            pltpu.VMEM((n, q, rows), BF),
            pltpu.VMEM((n, q, rows), BF),
            pltpu.VMEM((8, rows), F32),
            pltpu.VMEM((n, 8, rows), F32),
            pltpu.SemaphoreType.DMA((9,)),
            pltpu.SemaphoreType.DMA((9,)),
        ],
        compiler_params=pltpu.CompilerParams(
            collective_id=1, has_side_effects=True, vmem_limit_bytes=48 * 2**20
        ),
    )(blended, wo, odm, hidden, mask, oum, gain)


def shift_of(j):
    s, dx = j // PER, j % PER
    return dx, (dx + s // 2) % 4, s % 2


def shifted(c, j, way):
    dx, dy, dk = shift_of(j)
    x, y, k = c // 8, (c // 2) % 4, c % 2
    return (((x + way * dx + 4) % 4) * 4 + (y + way * dy + 4) % 4) * 2 + (k + dk) % 2


def expert_kernel(
    slots, d_ref, g_ref, e_ref, mi_ref, resid_ref, wg_hbm, wu_hbm, wd_hbm,
    out_ref, spread_ref,
    mi_nb, stg, xb, wg, wu, wd, raw, yo, ys, yr, ans, macc, m1s, m1r, pk,
    w_sem, mi_sem, ds, dr, zs, zr, ps, pr, bs, br, own_sem, m_sem, ks, kr, ss, sr,
):
    z, n, c, m = place()
    span = PER * slots
    q = mi_ref.shape[0]

    def step(ch):
        return 1 + 2 * lax.rem(c + ch, 2)

    def near(ch):
        return lax.rem(z + step(ch), n)

    def away(ch):
        return lax.rem(z + 4 - step(ch), n)

    def quarters(ch):
        return z, away(ch), near(ch), lax.rem(z + 2, n)

    barrier = pltpu.get_barrier_semaphore()

    @pl.loop(1, m)
    def _(j):
        pl.semaphore_signal(barrier, inc=1, device_id=(z, lax.rem(c + j, m)), device_id_type=MESH)

    for o in (1, 2, 3):
        pl.semaphore_signal(barrier, inc=1, device_id=(lax.rem(z + o, n), c), device_id_type=MESH)
    pl.semaphore_wait(barrier, m + 2)
    first = send(mi_ref, mi_nb, mi_sem.at[0], mi_sem.at[1], (near(0), c))

    def block(j):
        return pl.ds(pl.multiple_of(j * slots, slots), slots)

    def chunk(ch):
        return pl.ds(pl.multiple_of(ch * span, span), span)

    def sent_in_plane(ring, sem, r, ch):
        @pl.when(ch == 0)
        def _():
            wait_bytes(ring.at[r, 0, pl.ds(0, span - slots)], sem.at[r, ch])

        @pl.when(ch != 0)
        def _():
            wait_bytes(ring.at[r, 0], sem.at[r, ch])

    def others(ch):
        return 1 - (ch + CHUNKS - 1) // CHUNKS

    def dispatch(ch, r):
        slot = lax.rem(ch, SENDING)
        source = mi_ref if r == 0 else mi_nb

        @pl.when(ch >= SENDING)
        def _():
            sent_in_plane(stg, ds, r, ch - SENDING)

        stg[r, slot] = dot_nt(d_ref[chunk(ch)], source[...]).astype(BF)

        @pl.loop(others(ch), PER)
        def _(a):
            j = ch * PER + a
            send(stg.at[r, slot, block(a)], xb.at[r, block(j)], ds.at[r, ch], dr.at[r, ch], (z, shifted(c, j, 1)))

        @pl.when(ch == 0)
        def _():
            xb[r, :slots] = stg[r, 0, :slots]

    def came_in_plane(buffer, sem, r, ch):
        @pl.when(ch == 0)
        def _():
            wait_bytes(buffer.at[r, pl.ds(slots, span - slots)], sem.at[r, ch])

        @pl.when(ch != 0)
        def _():
            wait_bytes(buffer.at[r, chunk(ch)], sem.at[r, ch])

    def forward(ch):
        came_in_plane(xb, dr, 0, ch)
        send(xb.at[0, chunk(ch)], xb.at[2, chunk(ch)], zs.at[0, ch], zr.at[0, ch], (away(ch), c))
        came_in_plane(xb, dr, 1, ch)
        send(xb.at[1, chunk(ch)], xb.at[3, chunk(ch)], zs.at[1, ch], zr.at[1, ch], (near(ch), c))

    def experts(ch):
        slot = lax.rem(ch, RING)
        at = chunk(ch)
        names = quarters(ch)

        def rows_of(r):
            return pl.ds(pl.multiple_of(names[r] * q, 16), q)

        for r in range(2):
            wait_bytes(xb.at[r + 2, at], zr.at[r, ch])

            @pl.when(ch >= RING)
            def _():
                wait_bytes(ys.at[r, 0], ps.at[r, ch - RING])
                sent_in_plane(yo, bs, r, ch - RING)

        gate = dot(xb[0, at], wg[rows_of(0)])
        for r in range(1, 4):
            gate = gate + dot(xb[r, at], wg[rows_of(r)])
        lift = dot(xb[0, at], wu[rows_of(0)])
        for r in range(1, 4):
            lift = lift + dot(xb[r, at], wu[rows_of(r)])
        act = (gate * jax.nn.sigmoid(glu_alpha * gate) * (lift + 1.0)).astype(BF)
        for r in range(2):
            ys[r, slot] = dot(act, wd[names[r + 2]]).astype(BF)
            send(ys.at[r, slot], yr.at[r, at], ps.at[r, ch], pr.at[r, ch], ((near(ch), away(ch))[r], c))
        for r in range(2):
            yo[r, slot] = dot(act, wd[names[r]]).astype(BF)

    def give_back(ch):
        slot = lax.rem(ch, RING)
        for r in range(2):
            wait_bytes(yr.at[r, chunk(ch)], pr.at[r, ch])
            yo[r, slot] = (yo[r, slot].astype(F32) + yr[r, chunk(ch)].astype(F32)).astype(BF)

            @pl.loop(others(ch), PER)
            def _(a):
                j = ch * PER + a
                send(yo.at[r, slot, block(a)], ans.at[r, block(j)], bs.at[r, ch], br.at[r, ch], (z, shifted(c, j, -1)))

            @pl.when(ch == 0)
            def _():
                ans[r, :slots] = yo[r, 0, :slots]

    def absorb(ch):
        for r in (1, 0):
            came_in_plane(ans, br, r, ch)
            macc[r] += dot(g_ref[:, chunk(ch)], ans[r, chunk(ch)])

    steps = [(w, h0, min(128, q - h0)) for w in range(3) for h0 in range(0, q, 128)]

    def fetch(i):
        w, h0, hs = steps[i]
        return pltpu.make_async_copy(
            (wg_hbm, wu_hbm, wd_hbm)[w].at[pl.ds(h0, hs)], raw.at[i % 2, pl.ds(0, hs)], w_sem.at[i % 2]
        )

    fetch(0).start()

    @pl.loop(0, EARLY)
    def _(ch):
        dispatch(ch, 0)

    macc[...] = jnp.zeros_like(macc)
    first.wait_recv()

    @pl.loop(0, EARLY)
    def _(ch):
        dispatch(ch, 1)

    for i, (w, h0, hs) in enumerate(steps):
        if i + 1 < len(steps):
            fetch(i + 1).start()
        fetch(i).wait()
        if w < 2:
            into = (wg, wu)[w]
            whole = 4 * q // 128

            @pl.loop(0, whole)
            def _(b):
                lanes = pl.ds(pl.multiple_of(b * 128, 128), 128)
                into[lanes, h0 : h0 + hs] = raw[i % 2, :hs, lanes].T

            rest = whole * 128
            if rest < 4 * q:
                into[rest : 4 * q, h0 : h0 + hs] = raw[i % 2, :hs, rest : 4 * q].T
        else:
            for f in range(4):
                wd[f, h0 : h0 + hs, :] = raw[i % 2, :hs, f * q : (f + 1) * q]

    @pl.loop(0, CHUNKS + AHEAD + BACK)
    def _(t):
        @pl.when(t < CHUNKS)
        def _():
            forward(t)

        @pl.when(t + EARLY < CHUNKS)
        def _():
            dispatch(t + EARLY, 0)
            dispatch(t + EARLY, 1)

        @pl.when((t >= AHEAD) & (t < CHUNKS + AHEAD))
        def _():
            experts(t - AHEAD)

        @pl.when(t >= AHEAD + BACK)
        def _():
            give_back(t - AHEAD - BACK)

        @pl.when(t >= AHEAD + BACK + ABSORB)
        def _():
            absorb(t - AHEAD - BACK - ABSORB)

    @pl.loop(CHUNKS - ABSORB, CHUNKS)
    def _(ch):
        absorb(ch)

    m1s[...] = macc[1].astype(BF)
    last = send(m1s, m1r, m_sem.at[0], m_sem.at[1], (away(0), c))
    last.wait_recv()
    moe = (macc[0] + m1r[...].astype(F32)).astype(BF)
    done = (resid_ref[...].astype(F32) + moe.T.astype(F32)).astype(BF)
    out_ref[...] = done

    ends = dot_nt(e_ref[...], done)
    ends = jnp.concatenate([ends, jnp.zeros((ends.shape[0], 768 - q), F32)], axis=1)
    piece = lax.broadcasted_iota(jnp.int32, (ends.shape[0], 256), 0) // REQS
    packed = jnp.where(piece == 0, ends[:, :256], jnp.where(piece == 1, ends[:, 256:512], ends[:, 512:]))
    pk[z] = packed.astype(BF)
    more = [send(pk.at[z], pk.at[z], ks.at[o - 1], kr.at[o - 1], (lax.rem(z + o, n), c)) for o in (2, 1, 3)]
    for copy in more:
        copy.wait_recv()
    chip, core = c // 2, c % 2
    own_ends = pltpu.make_async_copy(pk, spread_ref.at[core, chip], own_sem.at[0])
    own_ends.start()

    @pl.loop(1, m // 2)
    def _(j):
        there = (((chip // 4 + j // 4) % 4) * 4 + (chip + j) % 4) * 2 + core
        send(pk, spread_ref.at[core, chip], ss.at[0], sr.at[0], (z, there))

    own_ends.wait()
    wait_bytes(spread_ref.at[0, pl.ds(0, m // 2 - 1)], sr.at[0])
    pair = send(spread_ref.at[core], spread_ref.at[core], ss.at[1], sr.at[1], (z, chip * 2 + 1 - core))
    last.wait_send()
    first.wait_send()
    for copy in more:
        copy.wait_send()

    for r in range(2):
        for ch in range(CHUNKS):
            wait_bytes(xb.at[r, pl.ds(0, span)], zs.at[r, ch])
        for ch in range(CHUNKS - SENDING, CHUNKS):
            wait_bytes(stg.at[r, 0], ds.at[r, ch])
        for ch in range(CHUNKS - RING, CHUNKS):
            wait_bytes(ys.at[r, 0], ps.at[r, ch])
            wait_bytes(yo.at[r, 0], bs.at[r, ch])
    wait_bytes(spread_ref.at[0, pl.ds(0, m // 2 - 1)], ss.at[0])
    pair.wait_send()
    pair.wait_recv()


def experts_call(pick, weigh, choose, moe_in, resid, wg, wu, wd, slots):
    rows, tokens = pick.shape
    q, f = moe_in.shape[0], wg.shape[0]
    columns, groups = rows // slots, wg.shape[1] // q
    span = PER * slots
    dma = lambda *s: pltpu.SemaphoreType.DMA(s)
    big = lambda k: pltpu.VMEM((k, rows, q), BF)
    sending = pltpu.VMEM((2, SENDING, span, q), BF)
    ring = pltpu.VMEM((2, RING, span, q), BF)
    pair = dma(2, CHUNKS)
    return pl.pallas_call(
        functools.partial(expert_kernel, slots),
        out_shape=(
            jax.ShapeDtypeStruct((q, tokens), BF),
            jax.ShapeDtypeStruct((2, columns // 2, groups, 16, 256), BF),
        ),
        in_specs=[VMEM] * 5 + [ANY] * 3,
        out_specs=(VMEM, ANY),
        scratch_shapes=[
            pltpu.VMEM((q, tokens), BF),
            sending, big(4),
            pltpu.VMEM((groups * q, f), BF), pltpu.VMEM((groups * q, f), BF), pltpu.VMEM((groups, f, q), BF),
            pltpu.VMEM((2, 128, groups * q), BF),
            ring, ring, big(2), big(2),
            pltpu.VMEM((2, tokens, q), F32), pltpu.VMEM((tokens, q), BF), pltpu.VMEM((tokens, q), BF),
            pltpu.VMEM((groups, 16, 256), BF),
            dma(2), dma(2),
            pair, pair, pair, pair, pair, pair, pair, pair,
            dma(1), dma(2), dma(3), dma(3), dma(2), dma(2),
        ],
        compiler_params=pltpu.CompilerParams(
            collective_id=2, has_side_effects=True, vmem_limit_bytes=63 * 2**20
        ),
    )(pick, weigh, choose, moe_in, resid, wg, wu, wd)


def shards(
    hidden, segments, request_adapter, routes, expert_gates, attention_gain, joined_weight, sinks,
    attention_out_weight, joined_down_maps, joined_up_maps, output_down_maps, output_up_maps,
    expert_norm_gain, expert_gate_weight, expert_up_weight, expert_down_weight, closing_gain, vocabulary_weight,
):
    groups, columns = lax.axis_size("dp"), lax.axis_size("expert")
    z, c = lax.axis_index("dp"), lax.axis_index("expert")
    segment_row, adapter_row = segments[0], request_adapter[0]
    tokens, quarter = hidden.shape
    width = quarter * groups
    share = tokens // groups
    aux = jnp.concatenate(
        [routes[0].astype(BF), expert_gates[0], jnp.zeros((share, 128 - 2 * TOP), BF)], axis=1
    )
    hid4, aux4 = gather_z(hidden.T, aux)
    rows = hid4.reshape(width, tokens)

    wide = rows.astype(F32)
    mean_square = jnp.mean(wide * wide, axis=0, keepdims=True)
    normed = (wide * lax.rsqrt(mean_square + epsilon) * attention_gain[:, None]).astype(BF)
    ranks = joined_down_maps.shape[1]
    projected = dot_tn(joined_weight.reshape(width, -1), normed)
    low = dot_tn(joined_down_maps, normed).astype(BF)
    request_ids = jnp.arange(REQS, dtype=jnp.int32)
    hits = segment_row[None, :] == request_ids[:, None]
    adapter = jnp.sum(jnp.where(hits, adapter_row[:, None], 0), axis=0)
    mask = adapter[None, :] == (jnp.arange(ranks, dtype=jnp.int32) // ADAPTER_RANK)[:, None]
    low = jnp.where(mask, low, jnp.zeros_like(low))
    projected = projected + adapter_scale * dot_tn(joined_up_maps.reshape(ranks, -1), low)
    counter = jnp.arange(tokens, dtype=jnp.int32)
    starts = jnp.min(jnp.where(hits, counter[None, :], tokens), axis=1)
    positions = counter - jnp.sum(jnp.where(hits, starts[:, None], 0), axis=0)
    half = HEAD_SIZE // 2
    frequency = theta_base ** (-2.0 * jnp.arange(half, dtype=F32) / HEAD_SIZE)
    angles = frequency[:, None] * positions.astype(F32)[None, :]
    cosine, sine = jnp.cos(angles)[None], jnp.sin(angles)[None]
    projected = projected.reshape(QUERY_GROUP + 2, HEAD_SIZE, tokens)
    one, two = projected[: QUERY_GROUP + 1, :half], projected[: QUERY_GROUP + 1, half:]
    turned = jnp.concatenate([one * cosine - two * sine, two * cosine + one * sine], axis=1).astype(BF)
    queries, keys, values = turned[:QUERY_GROUP], turned[QUERY_GROUP], projected[QUERY_GROUP + 1].astype(BF)
    scores = jnp.einsum("ght,hs->gts", queries, keys, preferred_element_type=F32) * HEAD_SIZE ** (-0.5)
    allowed = (segment_row[:, None] == segment_row[None, :]) & (counter[None, :] <= counter[:, None])
    weights = jnp.where(allowed[None], jnp.exp(scores), 0.0)
    totals = jnp.sum(weights, axis=-1, keepdims=True) + jnp.exp(sinks).reshape(QUERY_GROUP, 1, 1)
    probs = (weights / totals).astype(BF)
    blended = jnp.einsum("hs,gts->ght", values, probs, preferred_element_type=F32)
    blended = blended.astype(BF).reshape(QUERY_GROUP * HEAD_SIZE, tokens)

    gain = lax.dynamic_slice_in_dim(expert_norm_gain, z * quarter, quarter)[:, None]
    resid, moe_in = out_project(
        blended, attention_out_weight.T, output_down_maps, hidden.T, mask.astype(F32), output_up_maps.T, gain
    )

    route_all = aux4[:, :, :TOP].reshape(tokens, TOP)
    gate_all = aux4[:, :, TOP : 2 * TOP].reshape(tokens, TOP)
    slots = CAP * groups
    targets = shifted(c, jnp.arange(columns, dtype=jnp.int32), 1).astype(BF)
    named = route_all[:, :, None] == targets[None, None, :]
    hit = jnp.any(named, axis=1)
    gate_of = jnp.sum(jnp.where(named, gate_all.astype(F32)[:, :, None], 0.0), axis=1)
    before = (counter[None, :] < counter[:, None]).astype(BF)
    rank = jnp.where(hit, dot(before, hit.astype(BF)), -1.0)
    slot_ids = jnp.arange(slots, dtype=F32)
    pick = (rank.T[:, None, :] == slot_ids[None, :, None]).astype(BF).reshape(columns * slots, tokens)
    weigh = jnp.where(rank[:, :, None] == slot_ids[None, None, :], gate_of[:, :, None], 0.0)
    weigh = weigh.astype(BF).reshape(tokens, columns * slots)
    last = jnp.max(jnp.where(hits, counter[None, :], -1), axis=1)
    choose = (counter[None, :] == last[:, None]).astype(BF)
    choose = jnp.concatenate([choose, choose, choose, jnp.zeros_like(choose)], axis=0)

    done, spread = experts_call(
        pick, weigh, choose, moe_in, resid, expert_gate_weight[0].T, expert_up_weight[0].T, expert_down_weight[0], slots
    )

    ends = spread[:, :, :, : 3 * REQS].reshape(2, columns // 2, groups, 3, REQS, 256)
    ends = jnp.transpose(ends, (1, 0, 4, 2, 3, 5)).reshape(columns * REQS, groups, 768)[:, :, :quarter]
    ends = ends.reshape(columns * REQS, width).astype(F32)
    mean_square = jnp.mean(ends * ends, axis=1, keepdims=True)
    ends = (ends * lax.rsqrt(mean_square + epsilon) * closing_gain).astype(BF)
    logits = dot(ends, vocabulary_weight)
    return done.T, logits


def solution(mesh):
    in_specs = (
        P("expert", "dp"),
        P("expert", None),
        P("expert", None),
        P("expert", "dp", None),
        P("expert", "dp", None),
        P(),
        P(None, "dp", None),
        P("dp"),
        P("dp", None),
        P(),
        P(None, "dp", None),
        P("dp", None),
        P(None, "dp"),
        P(),
        P("expert", None, "dp"),
        P("expert", None, "dp"),
        P("expert", "dp", None),
        P(),
        P(None, ("dp", "expert")),
    )
    out_specs = (P("expert", "dp"), P(None, ("dp", "expert")))
    return jax.shard_map(shards, mesh=mesh, in_specs=in_specs, out_specs=out_specs, check_vma=False)
```

```python
import functools

import jax
import jax.numpy as jnp
from jax import lax
from jax.experimental import pallas as pl
from jax.experimental.pallas import tpu as pltpu
from jax.sharding import PartitionSpec as P

HEAD_SIZE = 64
QUERY_GROUP = 8
TOP = 4
ADAPTER_RANK = 16
REQS = 4
CAP = 16
CHUNKS = 8
PER = 4
EARLY = 3
AHEAD = 2
NEXT = 2
BACK = 1
ABSORB = 2
SENDING = 4
RING = 3

epsilon = 1e-05
theta_base = 150000.0
adapter_scale = 2.0
glu_alpha = 1.702

MESH = pl.DeviceIdType.MESH
BF = jnp.bfloat16
F32 = jnp.float32
VMEM = pl.BlockSpec(memory_space=pltpu.VMEM)
ANY = pl.BlockSpec(memory_space=pl.ANY)


def dot(a, b):
    return jnp.dot(a, b, preferred_element_type=F32)


def dot_nt(a, b):
    return lax.dot_general(a, b, (((1,), (1,)), ((), ())), preferred_element_type=F32)


def dot_tn(a, b):
    return lax.dot_general(a, b, (((0,), (0,)), ((), ())), preferred_element_type=F32)


def place():
    z, n = lax.axis_index("dp"), lax.axis_size("dp")
    c, m = lax.axis_index("expert"), lax.axis_size("expert")
    return z, n, c, m


def greet_z(offsets):
    z, n, c, _ = place()
    barrier = pltpu.get_barrier_semaphore()
    for o in offsets:
        pl.semaphore_signal(barrier, inc=1, device_id=(lax.rem(z + o, n), c), device_id_type=MESH)
    pl.semaphore_wait(barrier, len(offsets))


def send(src, dst, send_sem, recv_sem, device):
    copy = pltpu.make_async_remote_copy(
        src_ref=src, dst_ref=dst, send_sem=send_sem, recv_sem=recv_sem, device_id=device, device_id_type=MESH
    )
    copy.start()
    return copy


def wait_bytes(ref, sem):
    pltpu.make_async_copy(ref, ref, sem).wait()


def gather_kernel(x_ref, a_ref, xo_ref, ao_ref, ss, rs, local):
    z, n, c, _ = place()
    greet_z((1, 2, 3))
    own = pltpu.make_async_copy(x_ref, xo_ref.at[z], local.at[0])
    own.start()
    own_a = pltpu.make_async_copy(a_ref, ao_ref.at[z], local.at[1])
    own_a.start()
    half = x_ref.shape[0] // 32 * 16
    zu, zd = lax.rem(z + 1, n), lax.rem(z + 3, n)
    up, down, far = (zu, c), (zd, c), (lax.rem(z + 2, n), c)
    lo, hi = pl.ds(0, half), pl.ds(half, x_ref.shape[0] - half)
    copies = [
        send(x_ref.at[lo], xo_ref.at[z, lo], ss.at[0], rs.at[0], up),
        send(x_ref.at[hi], xo_ref.at[z, hi], ss.at[1], rs.at[1], down),
        send(a_ref, ao_ref.at[z], ss.at[6], rs.at[6], up),
        send(a_ref, ao_ref.at[z], ss.at[7], rs.at[7], down),
        send(a_ref, ao_ref.at[z], ss.at[8], rs.at[8], far),
        send(x_ref.at[hi], xo_ref.at[z, hi], ss.at[2], rs.at[2], up),
        send(x_ref.at[lo], xo_ref.at[z, lo], ss.at[3], rs.at[3], down),
    ]
    copies[0].wait_recv()
    copies.append(send(xo_ref.at[zd, lo], xo_ref.at[zd, lo], ss.at[4], rs.at[4], up))
    copies[1].wait_recv()
    copies.append(send(xo_ref.at[zu, hi], xo_ref.at[zu, hi], ss.at[5], rs.at[5], down))
    for copy in copies[2:]:
        copy.wait_recv()
    for copy in copies:
        copy.wait_send()
    own.wait()
    own_a.wait()


def gather_z(hidden, aux):
    n = lax.axis_size("dp")
    return pl.pallas_call(
        gather_kernel,
        out_shape=(
            jax.ShapeDtypeStruct((n,) + hidden.shape, hidden.dtype),
            jax.ShapeDtypeStruct((n,) + aux.shape, aux.dtype),
        ),
        in_specs=[VMEM, VMEM],
        out_specs=(VMEM, VMEM),
        scratch_shapes=[
            pltpu.SemaphoreType.DMA((9,)),
            pltpu.SemaphoreType.DMA((9,)),
            pltpu.SemaphoreType.DMA((2,)),
        ],
        compiler_params=pltpu.CompilerParams(
            collective_id=0, has_side_effects=True, vmem_limit_bytes=32 * 2**20
        ),
    )(hidden, aux)


def out_kernel(
    b_ref, wo_ref, odm_ref, hid_ref, mask_ref, oum_ref, gain_ref, aux_ref, target_ref,
    resid_ref, moe_ref, pick_ref, weigh_ref,
    low_snd, low_rcv, snd, rcv, st_snd, st_rcv, ss, rs,
):
    z, n, c, _ = place()
    quarter = hid_ref.shape[0]
    blended = b_ref[...]

    def part(q):
        return dot(wo_ref[pl.ds(pl.multiple_of(q * quarter, 16), quarter)], blended).astype(BF)

    low = dot_tn(odm_ref[...], blended).astype(BF)
    low_snd[...] = low
    greet_z((1, 2, 3))
    copies = []
    for o in (2, 1, 3):
        q = lax.rem(z + o, n)
        snd[o - 1] = part(q)
        copies.append(send(snd.at[o - 1], rcv.at[o - 1], ss.at[o + 2], rs.at[o + 2], (q, c)))
        copies.append(send(low_snd, low_rcv.at[o - 1], ss.at[o - 1], rs.at[o - 1], (q, c)))
    total = hid_ref[...].astype(F32) + part(z).astype(F32)

    blocks, tokens = target_ref.shape[0], hid_ref.shape[1]
    slots = pick_ref.shape[0] // blocks
    aux = aux_ref[...]
    hit = jnp.zeros((blocks, tokens), F32)
    gate = jnp.zeros((blocks, tokens), F32)
    for k in range(TOP):
        same = aux[k : k + 1] == target_ref[:, :1]
        hit = jnp.where(same, 1.0, hit)
        gate = jnp.where(same, aux[TOP + k : TOP + k + 1], gate)
    before = lax.broadcasted_iota(jnp.int32, (tokens, tokens), 0) < lax.broadcasted_iota(jnp.int32, (tokens, tokens), 1)
    rank = jnp.where(hit > 0.5, dot(hit.astype(BF), before.astype(F32).astype(BF)), -1.0)
    ids = lax.broadcasted_iota(jnp.int32, (slots, tokens), 0).astype(F32)
    for j in range(blocks):
        here = ids == rank[j : j + 1]
        pick_ref[j * slots : (j + 1) * slots] = jnp.where(here, 1.0, 0.0).astype(BF)
        weigh_ref[j * slots : (j + 1) * slots] = jnp.where(here, gate[j : j + 1], 0.0).astype(BF)

    for copy in copies[1::2]:
        copy.wait_recv()
    low_sum = low.astype(F32)
    for k in range(3):
        low_sum = low_sum + low_rcv[k].astype(F32)
    picked = (low_sum * mask_ref[...]).astype(BF)
    total = total + adapter_scale * dot(oum_ref[...], picked)
    for copy in copies[0::2]:
        copy.wait_recv()
    for k in range(3):
        total = total + rcv[k].astype(F32)
    resid = total.astype(BF)
    resid_ref[...] = resid
    wide = resid.astype(F32)
    sums = jnp.sum(wide * wide, axis=0, keepdims=True)
    st_snd[...] = jnp.broadcast_to(sums, st_snd.shape)
    more = []
    for o in (2, 1, 3):
        more.append(send(st_snd, st_rcv.at[o - 1], ss.at[o + 5], rs.at[o + 5], (lax.rem(z + o, n), c)))
    for copy in more:
        copy.wait_recv()
    every = st_snd[...] + st_rcv[0] + st_rcv[1] + st_rcv[2]
    scale = lax.rsqrt(every / (4.0 * quarter) + epsilon)
    moe_ref[...] = (wide * scale[:1] * gain_ref[...]).astype(BF)
    for copy in copies + more:
        copy.wait_send()


def out_project(blended, wo, odm, hidden, mask, oum, gain, aux, targets, slots):
    q, rows = hidden.shape
    table = jax.ShapeDtypeStruct((targets.shape[0] * slots, rows), BF)
    n = 3
    return pl.pallas_call(
        out_kernel,
        out_shape=(jax.ShapeDtypeStruct((q, rows), BF), jax.ShapeDtypeStruct((q, rows), BF), table, table),
        in_specs=[VMEM] * 9,
        out_specs=(VMEM,) * 4,
        scratch_shapes=[
            pltpu.VMEM(mask.shape, BF),
            pltpu.VMEM((n,) + mask.shape, BF),
            pltpu.VMEM((n, q, rows), BF),
            pltpu.VMEM((n, q, rows), BF),
            pltpu.VMEM((8, rows), F32),
            pltpu.VMEM((n, 8, rows), F32),
            pltpu.SemaphoreType.DMA((9,)),
            pltpu.SemaphoreType.DMA((9,)),
        ],
        compiler_params=pltpu.CompilerParams(
            collective_id=1, has_side_effects=True, vmem_limit_bytes=48 * 2**20
        ),
    )(blended, wo, odm, hidden, mask, oum, gain, aux, targets)


def shift_of(j):
    s, dx = j // PER, j % PER
    return dx, (dx + s // 2) % 4, s % 2


def shifted(c, j, way):
    dx, dy, dk = shift_of(j)
    x, y, k = c // 8, (c // 2) % 4, c % 2
    return (((x + way * dx + 4) % 4) * 4 + (y + way * dy + 4) % 4) * 2 + (k + dk) % 2


def expert_kernel(
    slots, d_ref, g_ref, e_ref, mi_ref, resid_ref, wg_hbm, wu_hbm, wd_hbm,
    out_ref, spread_ref,
    mi_nb, stg, xb, wg, wu, wd, raw, yo, ys, yr, ans, macc, m1s, m1r, e1s, e1r, pk,
    w_sem, mi_sem, ds, dr, zs, zr, ps, pr, bs, br, own_sem, m_sem, ks, kr, ss, sr,
):
    z, n, c, m = place()
    span = PER * slots
    q = mi_ref.shape[0]

    def step(ch):
        return 1 + 2 * lax.rem(c + ch, 2)

    def near(ch):
        return lax.rem(z + step(ch), n)

    def away(ch):
        return lax.rem(z + 4 - step(ch), n)

    def quarters(ch):
        return z, away(ch), near(ch), lax.rem(z + 2, n)

    barrier = pltpu.get_barrier_semaphore()

    @pl.loop(1, m)
    def _(j):
        pl.semaphore_signal(barrier, inc=1, device_id=(z, lax.rem(c + j, m)), device_id_type=MESH)

    for o in (1, 2, 3):
        pl.semaphore_signal(barrier, inc=1, device_id=(lax.rem(z + o, n), c), device_id_type=MESH)
    pl.semaphore_wait(barrier, m + 2)
    first = send(mi_ref, mi_nb, mi_sem.at[0], mi_sem.at[1], (near(0), c))

    def block(j):
        return pl.ds(pl.multiple_of(j * slots, slots), slots)

    def chunk(ch):
        return pl.ds(pl.multiple_of(ch * span, span), span)

    def sent_in_plane(ring, sem, r, ch):
        @pl.when(ch == 0)
        def _():
            wait_bytes(ring.at[r, 0, pl.ds(0, span - slots)], sem.at[r, ch])

        @pl.when(ch != 0)
        def _():
            wait_bytes(ring.at[r, 0], sem.at[r, ch])

    def others(ch):
        return 1 - (ch + CHUNKS - 1) // CHUNKS

    def dispatch(ch, r):
        slot = lax.rem(ch, SENDING)
        source = mi_ref if r == 0 else mi_nb

        @pl.when(ch >= SENDING)
        def _():
            sent_in_plane(stg, ds, r, ch - SENDING)

        stg[r, slot] = dot_nt(d_ref[chunk(ch)], source[...]).astype(BF)

        @pl.loop(others(ch), PER)
        def _(a):
            j = ch * PER + a
            send(stg.at[r, slot, block(a)], xb.at[r, block(j)], ds.at[r, ch], dr.at[r, ch], (z, shifted(c, j, 1)))

        @pl.when(ch == 0)
        def _():
            xb[r, :slots] = stg[r, 0, :slots]

    def came_in_plane(buffer, sem, r, ch):
        @pl.when(ch == 0)
        def _():
            wait_bytes(buffer.at[r, pl.ds(slots, span - slots)], sem.at[r, ch])

        @pl.when(ch != 0)
        def _():
            wait_bytes(buffer.at[r, chunk(ch)], sem.at[r, ch])

    def forward(ch, r):
        came_in_plane(xb, dr, r, ch)
        there = (away(ch), near(ch))[r]
        send(xb.at[r, chunk(ch)], xb.at[r + 2, chunk(ch)], zs.at[r, ch], zr.at[r, ch], (there, c))

    def experts(ch):
        slot = lax.rem(ch, RING)
        at = chunk(ch)
        names = quarters(ch)

        def rows_of(r):
            return pl.ds(pl.multiple_of(names[r] * q, 16), q)

        for r in range(2):
            wait_bytes(xb.at[r + 2, at], zr.at[r, ch])

            @pl.when(ch >= RING)
            def _():
                wait_bytes(ys.at[r, 0], ps.at[r, ch - RING])
                sent_in_plane(yo, bs, r, ch - RING)

        gate = dot(xb[0, at], wg[rows_of(0)])
        for r in range(1, 4):
            gate = gate + dot(xb[r, at], wg[rows_of(r)])
        lift = dot(xb[0, at], wu[rows_of(0)])
        for r in range(1, 4):
            lift = lift + dot(xb[r, at], wu[rows_of(r)])
        act = (gate * jax.nn.sigmoid(glu_alpha * gate) * (lift + 1.0)).astype(BF)
        for r in range(2):
            ys[r, slot] = dot(act, wd[names[r + 2]]).astype(BF)
            send(ys.at[r, slot], yr.at[r, at], ps.at[r, ch], pr.at[r, ch], ((near(ch), away(ch))[r], c))
        for r in range(2):
            yo[r, slot] = dot(act, wd[names[r]]).astype(BF)

    def give_back(ch):
        slot = lax.rem(ch, RING)
        for r in range(2):
            wait_bytes(yr.at[r, chunk(ch)], pr.at[r, ch])
            yo[r, slot] = (yo[r, slot].astype(F32) + yr[r, chunk(ch)].astype(F32)).astype(BF)

            @pl.loop(others(ch), PER)
            def _(a):
                j = ch * PER + a
                send(yo.at[r, slot, block(a)], ans.at[r, block(j)], bs.at[r, ch], br.at[r, ch], (z, shifted(c, j, -1)))

            @pl.when(ch == 0)
            def _():
                ans[r, :slots] = yo[r, 0, :slots]

    def absorb(ch):
        for r in (1, 0):
            came_in_plane(ans, br, r, ch)
            macc[r] += dot_tn(g_ref[chunk(ch)], ans[r, chunk(ch)])

    steps = [(w, h0, min(128, q - h0)) for w in range(3) for h0 in range(0, q, 128)]

    def fetch(i):
        w, h0, hs = steps[i]
        return pltpu.make_async_copy(
            (wg_hbm, wu_hbm, wd_hbm)[w].at[pl.ds(h0, hs)], raw.at[i % 2, pl.ds(0, hs)], w_sem.at[i % 2]
        )

    fetch(0).start()

    head = 2

    @pl.loop(0, head)
    def _(ch):
        dispatch(ch, 0)

    macc[...] = jnp.zeros_like(macc)
    first.wait_recv()

    @pl.loop(0, head)
    def _(ch):
        dispatch(ch, 1)

    @pl.loop(head, EARLY)
    def _(ch):
        dispatch(ch, 0)
        dispatch(ch, 1)

    for i, (w, h0, hs) in enumerate(steps):
        if i == len(steps) // 3:

            @pl.loop(0, AHEAD)
            def _(ch):
                forward(ch, 0)

        if i == 2 * len(steps) // 3:

            @pl.loop(0, NEXT)
            def _(ch):
                forward(ch, 1)

        if i + 1 < len(steps):
            fetch(i + 1).start()
        fetch(i).wait()
        if w < 2:
            into = (wg, wu)[w]
            whole = 4 * q // 128

            @pl.loop(0, whole)
            def _(b):
                lanes = pl.ds(pl.multiple_of(b * 128, 128), 128)
                into[lanes, h0 : h0 + hs] = raw[i % 2, :hs, lanes].T

            rest = whole * 128
            if rest < 4 * q:
                into[rest : 4 * q, h0 : h0 + hs] = raw[i % 2, :hs, rest : 4 * q].T
        else:
            for f in range(4):
                wd[f, h0 : h0 + hs, :] = raw[i % 2, :hs, f * q : (f + 1) * q]

    @pl.loop(0, CHUNKS + BACK)
    def _(t):
        @pl.when(t + AHEAD < CHUNKS)
        def _():
            forward(t + AHEAD, 0)

        @pl.when(t + NEXT < CHUNKS)
        def _():
            forward(t + NEXT, 1)

        @pl.when(t + EARLY < CHUNKS)
        def _():
            dispatch(t + EARLY, 0)
            dispatch(t + EARLY, 1)

        @pl.when(t < CHUNKS)
        def _():
            experts(t)

        @pl.when(t >= BACK)
        def _():
            give_back(t - BACK)

        @pl.when(t >= BACK + ABSORB)
        def _():
            absorb(t - BACK - ABSORB)

    @pl.loop(CHUNKS - ABSORB, CHUNKS)
    def _(ch):
        absorb(ch)

    m1s[...] = macc[1].astype(BF)
    e1s[...] = dot(e_ref[...], m1s[...]).astype(BF)
    hasty = send(e1s, e1r, m_sem.at[2], m_sem.at[3], (away(0), c))
    last = send(m1s, m1r, m_sem.at[0], m_sem.at[1], (away(0), c))
    ends = jnp.dot(e_ref[...].astype(F32), macc[0], preferred_element_type=F32, precision=lax.Precision.HIGHEST)
    kept = dot_nt(e_ref[...], resid_ref[...])
    hasty.wait_recv()
    ends = kept + (ends + e1r[...].astype(F32)).astype(BF).astype(F32)
    ends = jnp.concatenate([ends, jnp.zeros((ends.shape[0], 768 - q), F32)], axis=1)
    piece = lax.broadcasted_iota(jnp.int32, (ends.shape[0], 256), 0) // REQS
    packed = jnp.where(piece == 0, ends[:, :256], jnp.where(piece == 1, ends[:, 256:512], ends[:, 512:]))
    pk[z] = packed.astype(BF)
    more = [send(pk.at[z], pk.at[z], ks.at[o - 1], kr.at[o - 1], (lax.rem(z + o, n), c)) for o in (2, 1, 3)]
    for copy in more:
        copy.wait_recv()
    chip, core = c // 2, c % 2
    own_ends = pltpu.make_async_copy(pk, spread_ref.at[core, chip], own_sem.at[0])
    own_ends.start()

    @pl.loop(1, m // 2)
    def _(j):
        there = (((chip // 4 + j // 4) % 4) * 4 + (chip + j) % 4) * 2 + core
        send(pk, spread_ref.at[core, chip], ss.at[0], sr.at[0], (z, there))

    last.wait_recv()
    moe = (macc[0] + m1r[...].astype(F32)).astype(BF)
    out_ref[...] = (resid_ref[...].astype(F32) + moe.T.astype(F32)).astype(BF)
    own_ends.wait()
    wait_bytes(spread_ref.at[0, pl.ds(0, m // 2 - 1)], sr.at[0])
    pair = send(spread_ref.at[core], spread_ref.at[core], ss.at[1], sr.at[1], (z, chip * 2 + 1 - core))
    last.wait_send()
    hasty.wait_send()
    first.wait_send()
    for copy in more:
        copy.wait_send()

    for r in range(2):
        for ch in range(CHUNKS):
            wait_bytes(xb.at[r, pl.ds(0, span)], zs.at[r, ch])
        for ch in range(CHUNKS - SENDING, CHUNKS):
            wait_bytes(stg.at[r, 0], ds.at[r, ch])
        for ch in range(CHUNKS - RING, CHUNKS):
            wait_bytes(ys.at[r, 0], ps.at[r, ch])
            wait_bytes(yo.at[r, 0], bs.at[r, ch])
    wait_bytes(spread_ref.at[0, pl.ds(0, m // 2 - 1)], ss.at[0])
    pair.wait_send()
    pair.wait_recv()


def experts_call(pick, weigh, choose, moe_in, resid, wg, wu, wd, slots):
    rows, tokens = pick.shape
    q, f = moe_in.shape[0], wg.shape[0]
    columns, groups = rows // slots, wg.shape[1] // q
    span = PER * slots
    dma = lambda *s: pltpu.SemaphoreType.DMA(s)
    big = lambda k: pltpu.VMEM((k, rows, q), BF)
    sending = pltpu.VMEM((2, SENDING, span, q), BF)
    ring = pltpu.VMEM((2, RING, span, q), BF)
    pair = dma(2, CHUNKS)
    return pl.pallas_call(
        functools.partial(expert_kernel, slots),
        out_shape=(
            jax.ShapeDtypeStruct((q, tokens), BF),
            jax.ShapeDtypeStruct((2, columns // 2, groups, 16, 256), BF),
        ),
        in_specs=[VMEM] * 5 + [ANY] * 3,
        out_specs=(VMEM, ANY),
        scratch_shapes=[
            pltpu.VMEM((q, tokens), BF),
            sending, big(4),
            pltpu.VMEM((groups * q, f), BF), pltpu.VMEM((groups * q, f), BF), pltpu.VMEM((groups, f, q), BF),
            pltpu.VMEM((2, 128, groups * q), BF),
            ring, ring, big(2), big(2),
            pltpu.VMEM((2, tokens, q), F32), pltpu.VMEM((tokens, q), BF), pltpu.VMEM((tokens, q), BF),
            pltpu.VMEM((16, q), BF), pltpu.VMEM((16, q), BF),
            pltpu.VMEM((groups, 16, 256), BF),
            dma(2), dma(2),
            pair, pair, pair, pair, pair, pair, pair, pair,
            dma(1), dma(4), dma(3), dma(3), dma(2), dma(2),
        ],
        compiler_params=pltpu.CompilerParams(
            collective_id=2, has_side_effects=True, vmem_limit_bytes=63 * 2**20
        ),
    )(pick, weigh, choose, moe_in, resid, wg, wu, wd)


def shards(
    hidden, segments, request_adapter, routes, expert_gates, attention_gain, joined_weight, sinks,
    attention_out_weight, joined_down_maps, joined_up_maps, output_down_maps, output_up_maps,
    expert_norm_gain, expert_gate_weight, expert_up_weight, expert_down_weight, closing_gain, vocabulary_weight,
):
    groups, columns = lax.axis_size("dp"), lax.axis_size("expert")
    z, c = lax.axis_index("dp"), lax.axis_index("expert")
    segment_row, adapter_row = segments[0], request_adapter[0]
    tokens, quarter = hidden.shape
    width = quarter * groups
    share = tokens // groups
    aux = jnp.concatenate([routes[0].T.astype(BF), expert_gates[0].T], axis=0)
    aux = jnp.pad(aux, ((0, 16 - 2 * TOP), (0, 128 - share)))
    hid4, aux4 = gather_z(hidden.T, aux)
    rows = hid4.reshape(width, tokens)

    wide = rows.astype(F32)
    mean_square = jnp.mean(wide * wide, axis=0, keepdims=True)
    normed = (wide * lax.rsqrt(mean_square + epsilon) * attention_gain[:, None]).astype(BF)
    ranks = joined_down_maps.shape[1]
    projected = dot_tn(joined_weight.reshape(width, -1), normed)
    low = dot_tn(joined_down_maps, normed).astype(BF)
    request_ids = jnp.arange(REQS, dtype=jnp.int32)
    hits = segment_row[None, :] == request_ids[:, None]
    adapter = jnp.sum(jnp.where(hits, adapter_row[:, None], 0), axis=0)
    mask = adapter[None, :] == (jnp.arange(ranks, dtype=jnp.int32) // ADAPTER_RANK)[:, None]
    low = jnp.where(mask, low, jnp.zeros_like(low))
    projected = projected + adapter_scale * dot_tn(joined_up_maps.reshape(ranks, -1), low)
    counter = jnp.arange(tokens, dtype=jnp.int32)
    starts = jnp.min(jnp.where(hits, counter[None, :], tokens), axis=1)
    positions = counter - jnp.sum(jnp.where(hits, starts[:, None], 0), axis=0)
    half = HEAD_SIZE // 2
    frequency = theta_base ** (-2.0 * jnp.arange(half, dtype=F32) / HEAD_SIZE)
    angles = frequency[:, None] * positions.astype(F32)[None, :]
    cosine, sine = jnp.cos(angles)[None], jnp.sin(angles)[None]
    projected = projected.reshape(QUERY_GROUP + 2, HEAD_SIZE, tokens)
    one, two = projected[: QUERY_GROUP + 1, :half], projected[: QUERY_GROUP + 1, half:]
    turned = jnp.concatenate([one * cosine - two * sine, two * cosine + one * sine], axis=1).astype(BF)
    queries, keys, values = turned[:QUERY_GROUP], turned[QUERY_GROUP], projected[QUERY_GROUP + 1].astype(BF)
    scores = jnp.einsum("ght,hs->gts", queries, keys, preferred_element_type=F32) * HEAD_SIZE ** (-0.5)
    allowed = (segment_row[:, None] == segment_row[None, :]) & (counter[None, :] <= counter[:, None])
    weights = jnp.where(allowed[None], jnp.exp(scores), 0.0)
    totals = jnp.sum(weights, axis=-1, keepdims=True) + jnp.exp(sinks).reshape(QUERY_GROUP, 1, 1)
    probs = (weights / totals).astype(BF)
    blended = jnp.einsum("hs,gts->ght", values, probs, preferred_element_type=F32)
    blended = blended.astype(BF).reshape(QUERY_GROUP * HEAD_SIZE, tokens)

    gain = lax.dynamic_slice_in_dim(expert_norm_gain, z * quarter, quarter)[:, None]
    slots = CAP * groups
    aux = jnp.transpose(aux4[:, :, :share], (1, 0, 2)).reshape(16, tokens).astype(F32)
    targets = shifted(c, jnp.arange(columns, dtype=jnp.int32), 1).astype(F32)
    targets = jnp.broadcast_to(targets[:, None], (columns, 128))
    resid, moe_in, pick, weigh = out_project(
        blended, attention_out_weight.T, output_down_maps, hidden.T, mask.astype(F32), output_up_maps.T, gain,
        aux, targets, slots
    )
    last = jnp.max(jnp.where(hits, counter[None, :], -1), axis=1)
    choose = (counter[None, :] == last[:, None]).astype(BF)
    choose = jnp.concatenate([choose, choose, choose, jnp.zeros_like(choose)], axis=0)

    done, spread = experts_call(
        pick, weigh, choose, moe_in, resid, expert_gate_weight[0].T, expert_up_weight[0].T, expert_down_weight[0], slots
    )

    ends = spread[:, :, :, : 3 * REQS].reshape(2, columns // 2, groups, 3, REQS, 256)
    ends = jnp.transpose(ends, (1, 0, 4, 2, 3, 5)).reshape(columns * REQS, groups, 768)[:, :, :quarter]
    ends = ends.reshape(columns * REQS, width).astype(F32)
    mean_square = jnp.mean(ends * ends, axis=1, keepdims=True)
    ends = (ends * lax.rsqrt(mean_square + epsilon) * closing_gain).astype(BF)
    logits = dot(ends, vocabulary_weight)
    return done.T, logits


def solution(mesh):
    in_specs = (
        P("expert", "dp"),
        P("expert", None),
        P("expert", None),
        P("expert", "dp", None),
        P("expert", "dp", None),
        P(),
        P(None, "dp", None),
        P("dp"),
        P("dp", None),
        P(),
        P(None, "dp", None),
        P("dp", None),
        P(None, "dp"),
        P(),
        P("expert", None, "dp"),
        P("expert", None, "dp"),
        P("expert", "dp", None),
        P(),
        P(None, ("dp", "expert")),
    )
    out_specs = (P("expert", "dp"), P(None, ("dp", "expert")))
    return jax.shard_map(shards, mesh=mesh, in_specs=in_specs, out_specs=out_specs, check_vma=False)
```

```python
import functools

import jax
import jax.numpy as jnp
from jax import lax
from jax.experimental import pallas as pl
from jax.experimental.pallas import tpu as pltpu
from jax.sharding import PartitionSpec as P

HEAD_SIZE = 64
QUERY_GROUP = 8
TOP = 4
ADAPTER_RANK = 16
REQS = 4
CAP = 16
CHUNKS = 8
PER = 4
EARLY = 3
AHEAD = 2
NEXT = 2
BACK = 1
ABSORB = 2
SENDING = 4
RING = 3

epsilon = 1e-05
theta_base = 150000.0
adapter_scale = 2.0
glu_alpha = 1.702

MESH = pl.DeviceIdType.MESH
BF = jnp.bfloat16
F32 = jnp.float32
VMEM = pl.BlockSpec(memory_space=pltpu.VMEM)
ANY = pl.BlockSpec(memory_space=pl.ANY)


def dot(a, b):
    return jnp.dot(a, b, preferred_element_type=F32)


def dot_nt(a, b):
    return lax.dot_general(a, b, (((1,), (1,)), ((), ())), preferred_element_type=F32)


def dot_tn(a, b):
    return lax.dot_general(a, b, (((0,), (0,)), ((), ())), preferred_element_type=F32)


def place():
    z, n = lax.axis_index("dp"), lax.axis_size("dp")
    c, m = lax.axis_index("expert"), lax.axis_size("expert")
    return z, n, c, m


def greet_z(offsets):
    z, n, c, _ = place()
    barrier = pltpu.get_barrier_semaphore()
    for o in offsets:
        pl.semaphore_signal(barrier, inc=1, device_id=(lax.rem(z + o, n), c), device_id_type=MESH)
    pl.semaphore_wait(barrier, len(offsets))


def send(src, dst, send_sem, recv_sem, device):
    copy = pltpu.make_async_remote_copy(
        src_ref=src, dst_ref=dst, send_sem=send_sem, recv_sem=recv_sem, device_id=device, device_id_type=MESH
    )
    copy.start()
    return copy


def wait_bytes(ref, sem):
    pltpu.make_async_copy(ref, ref, sem).wait()


def gather_kernel(x_ref, a_ref, xo_ref, ao_ref, ss, rs, local):
    z, n, c, _ = place()
    greet_z((1, 2, 3))
    own = pltpu.make_async_copy(x_ref, xo_ref.at[z], local.at[0])
    own.start()
    own_a = pltpu.make_async_copy(a_ref, ao_ref.at[z], local.at[1])
    own_a.start()
    half = x_ref.shape[0] // 32 * 16
    zu, zd = lax.rem(z + 1, n), lax.rem(z + 3, n)
    up, down, far = (zu, c), (zd, c), (lax.rem(z + 2, n), c)
    lo, hi = pl.ds(0, half), pl.ds(half, x_ref.shape[0] - half)
    copies = [
        send(x_ref.at[lo], xo_ref.at[z, lo], ss.at[0], rs.at[0], up),
        send(x_ref.at[hi], xo_ref.at[z, hi], ss.at[1], rs.at[1], down),
        send(a_ref, ao_ref.at[z], ss.at[6], rs.at[6], up),
        send(a_ref, ao_ref.at[z], ss.at[7], rs.at[7], down),
        send(a_ref, ao_ref.at[z], ss.at[8], rs.at[8], far),
        send(x_ref.at[hi], xo_ref.at[z, hi], ss.at[2], rs.at[2], up),
        send(x_ref.at[lo], xo_ref.at[z, lo], ss.at[3], rs.at[3], down),
    ]
    copies[0].wait_recv()
    copies.append(send(xo_ref.at[zd, lo], xo_ref.at[zd, lo], ss.at[4], rs.at[4], up))
    copies[1].wait_recv()
    copies.append(send(xo_ref.at[zu, hi], xo_ref.at[zu, hi], ss.at[5], rs.at[5], down))
    for copy in copies[2:]:
        copy.wait_recv()
    for copy in copies:
        copy.wait_send()
    own.wait()
    own_a.wait()


def gather_z(hidden, aux):
    n = lax.axis_size("dp")
    return pl.pallas_call(
        gather_kernel,
        out_shape=(
            jax.ShapeDtypeStruct((n,) + hidden.shape, hidden.dtype),
            jax.ShapeDtypeStruct((n,) + aux.shape, aux.dtype),
        ),
        in_specs=[VMEM, VMEM],
        out_specs=(VMEM, VMEM),
        scratch_shapes=[
            pltpu.SemaphoreType.DMA((9,)),
            pltpu.SemaphoreType.DMA((9,)),
            pltpu.SemaphoreType.DMA((2,)),
        ],
        compiler_params=pltpu.CompilerParams(
            collective_id=0, has_side_effects=True, vmem_limit_bytes=32 * 2**20
        ),
    )(hidden, aux)


def out_kernel(
    b_ref, wo_hbm, odm_hbm, hid_hbm, mask_ref, oum_hbm, gain_ref, aux_ref, target_ref,
    resid_ref, moe_ref, pick_ref, weigh_ref,
    wo_ref, odm_ref, hid_ref, oum_ref, low_snd, low_rcv, far, passed, snd, rcv, st_snd, st_rcv, fetch, ss, rs,
):
    z, n, c, _ = place()
    loads = [
        pltpu.make_async_copy(src, dst, fetch.at[i])
        for i, (src, dst) in enumerate(
            ((wo_hbm, wo_ref), (odm_hbm, odm_ref), (hid_hbm, hid_ref), (oum_hbm, oum_ref))
        )
    ]
    for load in loads:
        load.start()
    quarter = hid_ref.shape[0]
    half = quarter // 32 * 16
    lo, hi = pl.ds(0, half), pl.ds(half, quarter - half)
    zu, zf, zd = lax.rem(z + 1, n), lax.rem(z + 2, n), lax.rem(z + 3, n)
    up, down = (zu, c), (zd, c)
    blended = b_ref[...]

    def part(q):
        return dot(wo_ref[pl.ds(pl.multiple_of(q * quarter, 16), quarter)], blended)

    greet_z((1, 2, 3))
    loads[0].wait()
    far[...] = part(zf).astype(BF)
    relays = [
        send(far.at[lo], passed.at[lo], ss.at[3], rs.at[3], up),
        send(far.at[hi], passed.at[hi], ss.at[4], rs.at[4], down),
    ]
    above, below = part(zu), part(zd)
    snd[0, half:] = above[half:].astype(BF)
    snd[1, :half] = below[:half].astype(BF)
    shares = [
        send(snd.at[0, hi], rcv.at[0, hi], ss.at[5], rs.at[5], up),
        send(snd.at[1, lo], rcv.at[1, lo], ss.at[6], rs.at[6], down),
    ]
    loads[1].wait()
    low = dot_tn(odm_ref[...], blended).astype(BF)
    low_snd[...] = low
    lows = [
        send(low_snd, low_rcv.at[o - 1], ss.at[o - 1], rs.at[o - 1], (lax.rem(z + o, n), c)) for o in (2, 1, 3)
    ]
    relays[0].wait_recv()
    snd[0, :half] = (above[:half] + passed[:half].astype(F32)).astype(BF)
    shares.append(send(snd.at[0, lo], rcv.at[0, lo], ss.at[7], rs.at[7], up))
    relays[1].wait_recv()
    snd[1, half:] = (below[half:] + passed[half:].astype(F32)).astype(BF)
    shares.append(send(snd.at[1, hi], rcv.at[1, hi], ss.at[8], rs.at[8], down))
    for load in loads[2:]:
        load.wait()
    total = hid_ref[...].astype(F32) + part(z)

    blocks, tokens = target_ref.shape[0], hid_ref.shape[1]
    slots = pick_ref.shape[0] // blocks
    aux = aux_ref[...]
    hit = jnp.zeros((blocks, tokens), F32)
    gate = jnp.zeros((blocks, tokens), F32)
    for k in range(TOP):
        same = aux[k : k + 1] == target_ref[:, :1]
        hit = jnp.where(same, 1.0, hit)
        gate = jnp.where(same, aux[TOP + k : TOP + k + 1], gate)
    before = lax.broadcasted_iota(jnp.int32, (tokens, tokens), 0) < lax.broadcasted_iota(jnp.int32, (tokens, tokens), 1)
    rank = jnp.where(hit > 0.5, dot(hit.astype(BF), before.astype(F32).astype(BF)), -1.0)
    ids = lax.broadcasted_iota(jnp.int32, (slots, tokens), 0).astype(F32)
    for j in range(blocks):
        here = ids == rank[j : j + 1]
        pick_ref[j * slots : (j + 1) * slots] = jnp.where(here, 1.0, 0.0).astype(BF)
        weigh_ref[j * slots : (j + 1) * slots] = jnp.where(here, gate[j : j + 1], 0.0).astype(BF)

    for copy in lows:
        copy.wait_recv()
    low_sum = low.astype(F32)
    for k in range(3):
        low_sum = low_sum + low_rcv[k].astype(F32)
    picked = (low_sum * mask_ref[...]).astype(BF)
    total = total + adapter_scale * dot(oum_ref[...], picked)
    for copy in shares:
        copy.wait_recv()
    total = total + rcv[0].astype(F32) + rcv[1].astype(F32)
    resid = total.astype(BF)
    resid_ref[...] = resid
    wide = resid.astype(F32)
    sums = jnp.sum(wide * wide, axis=0, keepdims=True)
    st_snd[...] = jnp.broadcast_to(sums, st_snd.shape)
    more = []
    for o in (2, 1, 3):
        more.append(send(st_snd, st_rcv.at[o - 1], ss.at[o + 8], rs.at[o + 8], (lax.rem(z + o, n), c)))
    for copy in more:
        copy.wait_recv()
    every = st_snd[...] + st_rcv[0] + st_rcv[1] + st_rcv[2]
    scale = lax.rsqrt(every / (4.0 * quarter) + epsilon)
    moe_ref[...] = (wide * scale[:1] * gain_ref[...]).astype(BF)
    for copy in relays + shares + lows + more:
        copy.wait_send()


def out_project(blended, wo, odm, hidden, mask, oum, gain, aux, targets, slots):
    q, rows = hidden.shape
    table = jax.ShapeDtypeStruct((targets.shape[0] * slots, rows), BF)
    n = 3
    return pl.pallas_call(
        out_kernel,
        out_shape=(jax.ShapeDtypeStruct((q, rows), BF), jax.ShapeDtypeStruct((q, rows), BF), table, table),
        in_specs=[VMEM, ANY, ANY, ANY, VMEM, ANY, VMEM, VMEM, VMEM],
        out_specs=(VMEM,) * 4,
        scratch_shapes=[
            pltpu.VMEM(wo.shape, BF),
            pltpu.VMEM(odm.shape, BF),
            pltpu.VMEM(hidden.shape, BF),
            pltpu.VMEM(oum.shape, BF),
            pltpu.VMEM(mask.shape, BF),
            pltpu.VMEM((n,) + mask.shape, BF),
            pltpu.VMEM((q, rows), BF),
            pltpu.VMEM((q, rows), BF),
            pltpu.VMEM((2, q, rows), BF),
            pltpu.VMEM((2, q, rows), BF),
            pltpu.VMEM((8, rows), F32),
            pltpu.VMEM((n, 8, rows), F32),
            pltpu.SemaphoreType.DMA((4,)),
            pltpu.SemaphoreType.DMA((12,)),
            pltpu.SemaphoreType.DMA((12,)),
        ],
        compiler_params=pltpu.CompilerParams(
            collective_id=1, has_side_effects=True, vmem_limit_bytes=48 * 2**20
        ),
    )(blended, wo, odm, hidden, mask, oum, gain, aux, targets)


def shift_of(j):
    s, dx = j // PER, j % PER
    return dx, (dx + s // 2) % 4, s % 2


def shifted(c, j, way):
    dx, dy, dk = shift_of(j)
    x, y, k = c // 8, (c // 2) % 4, c % 2
    return (((x + way * dx + 4) % 4) * 4 + (y + way * dy + 4) % 4) * 2 + (k + dk) % 2


def expert_kernel(
    slots, d_hbm, g_hbm, e_ref, mi_hbm, resid_hbm, wg_hbm, wu_hbm, wd_hbm,
    out_ref, spread_ref,
    d_ref, g_ref, mi_ref, resid_ref, fetched, mi_nb, stg, xb, wg, wu, wd, raw, yo, ys, yr, ans, macc, m1s, m1r, e1s, e1r, pk,
    w_sem, mi_sem, ds, dr, zs, zr, ps, pr, bs, br, own_sem, m_sem, ks, kr, ss, sr,
):
    z, n, c, m = place()
    loads = [
        pltpu.make_async_copy(src, dst, fetched.at[i])
        for i, (src, dst) in enumerate(((mi_hbm, mi_ref), (d_hbm, d_ref), (g_hbm, g_ref), (resid_hbm, resid_ref)))
    ]
    for load in loads:
        load.start()
    span = PER * slots
    q = mi_ref.shape[0]

    def step(ch):
        return 1 + 2 * lax.rem(c + ch, 2)

    def near(ch):
        return lax.rem(z + step(ch), n)

    def away(ch):
        return lax.rem(z + 4 - step(ch), n)

    def quarters(ch):
        return z, away(ch), near(ch), lax.rem(z + 2, n)

    barrier = pltpu.get_barrier_semaphore()

    @pl.loop(1, m)
    def _(j):
        pl.semaphore_signal(barrier, inc=1, device_id=(z, lax.rem(c + j, m)), device_id_type=MESH)

    for o in (1, 2, 3):
        pl.semaphore_signal(barrier, inc=1, device_id=(lax.rem(z + o, n), c), device_id_type=MESH)
    pl.semaphore_wait(barrier, m + 2)
    loads[0].wait()
    first = send(mi_ref, mi_nb, mi_sem.at[0], mi_sem.at[1], (near(0), c))

    def block(j):
        return pl.ds(pl.multiple_of(j * slots, slots), slots)

    def chunk(ch):
        return pl.ds(pl.multiple_of(ch * span, span), span)

    def sent_in_plane(ring, sem, r, ch):
        @pl.when(ch == 0)
        def _():
            wait_bytes(ring.at[r, 0, pl.ds(0, span - slots)], sem.at[r, ch])

        @pl.when(ch != 0)
        def _():
            wait_bytes(ring.at[r, 0], sem.at[r, ch])

    def others(ch):
        return 1 - (ch + CHUNKS - 1) // CHUNKS

    def dispatch(ch, r):
        slot = lax.rem(ch, SENDING)
        source = mi_ref if r == 0 else mi_nb

        @pl.when(ch >= SENDING)
        def _():
            sent_in_plane(stg, ds, r, ch - SENDING)

        stg[r, slot] = dot_nt(d_ref[chunk(ch)], source[...]).astype(BF)

        @pl.loop(others(ch), PER)
        def _(a):
            j = ch * PER + a
            send(stg.at[r, slot, block(a)], xb.at[r, block(j)], ds.at[r, ch], dr.at[r, ch], (z, shifted(c, j, 1)))

        @pl.when(ch == 0)
        def _():
            xb[r, :slots] = stg[r, 0, :slots]

    def came_in_plane(buffer, sem, r, ch):
        @pl.when(ch == 0)
        def _():
            wait_bytes(buffer.at[r, pl.ds(slots, span - slots)], sem.at[r, ch])

        @pl.when(ch != 0)
        def _():
            wait_bytes(buffer.at[r, chunk(ch)], sem.at[r, ch])

    def forward(ch, r):
        came_in_plane(xb, dr, r, ch)
        there = (away(ch), near(ch))[r]
        send(xb.at[r, chunk(ch)], xb.at[r + 2, chunk(ch)], zs.at[r, ch], zr.at[r, ch], (there, c))

    def experts(ch):
        slot = lax.rem(ch, RING)
        at = chunk(ch)
        names = quarters(ch)

        def rows_of(r):
            return pl.ds(pl.multiple_of(names[r] * q, 16), q)

        for r in range(2):
            wait_bytes(xb.at[r + 2, at], zr.at[r, ch])

            @pl.when(ch >= RING)
            def _():
                wait_bytes(ys.at[r, 0], ps.at[r, ch - RING])
                sent_in_plane(yo, bs, r, ch - RING)

        gate = dot(xb[0, at], wg[rows_of(0)])
        for r in range(1, 4):
            gate = gate + dot(xb[r, at], wg[rows_of(r)])
        lift = dot(xb[0, at], wu[rows_of(0)])
        for r in range(1, 4):
            lift = lift + dot(xb[r, at], wu[rows_of(r)])
        act = (gate * jax.nn.sigmoid(glu_alpha * gate) * (lift + 1.0)).astype(BF)
        for r in range(2):
            ys[r, slot] = dot(act, wd[names[r + 2]]).astype(BF)
            send(ys.at[r, slot], yr.at[r, at], ps.at[r, ch], pr.at[r, ch], ((near(ch), away(ch))[r], c))
        for r in range(2):
            yo[r, slot] = dot(act, wd[names[r]]).astype(BF)

    def give_back(ch):
        slot = lax.rem(ch, RING)
        for r in range(2):
            wait_bytes(yr.at[r, chunk(ch)], pr.at[r, ch])
            yo[r, slot] = (yo[r, slot].astype(F32) + yr[r, chunk(ch)].astype(F32)).astype(BF)

            @pl.loop(others(ch), PER)
            def _(a):
                j = ch * PER + a
                send(yo.at[r, slot, block(a)], ans.at[r, block(j)], bs.at[r, ch], br.at[r, ch], (z, shifted(c, j, -1)))

            @pl.when(ch == 0)
            def _():
                ans[r, :slots] = yo[r, 0, :slots]

    def absorb(ch):
        for r in (1, 0):
            came_in_plane(ans, br, r, ch)
            macc[r] += dot_tn(g_ref[chunk(ch)], ans[r, chunk(ch)])

    steps = [(w, h0, min(128, q - h0)) for w in range(3) for h0 in range(0, q, 128)]

    def fetch(i):
        w, h0, hs = steps[i]
        return pltpu.make_async_copy(
            (wg_hbm, wu_hbm, wd_hbm)[w].at[pl.ds(h0, hs)], raw.at[i % 2, pl.ds(0, hs)], w_sem.at[i % 2]
        )

    fetch(0).start()

    loads[1].wait()
    head = 2

    @pl.loop(0, head)
    def _(ch):
        dispatch(ch, 0)

    macc[...] = jnp.zeros_like(macc)
    loads[2].wait()
    loads[3].wait()
    first.wait_recv()

    @pl.loop(0, head)
    def _(ch):
        dispatch(ch, 1)

    @pl.loop(head, EARLY)
    def _(ch):
        dispatch(ch, 0)
        dispatch(ch, 1)

    for i, (w, h0, hs) in enumerate(steps):
        if i == len(steps) // 3:

            @pl.loop(0, AHEAD)
            def _(ch):
                forward(ch, 0)

        if i == 2 * len(steps) // 3:

            @pl.loop(0, NEXT)
            def _(ch):
                forward(ch, 1)

        if i + 1 < len(steps):
            fetch(i + 1).start()
        fetch(i).wait()
        if w < 2:
            into = (wg, wu)[w]
            whole = 4 * q // 128

            @pl.loop(0, whole)
            def _(b):
                lanes = pl.ds(pl.multiple_of(b * 128, 128), 128)
                into[lanes, h0 : h0 + hs] = raw[i % 2, :hs, lanes].T

            rest = whole * 128
            if rest < 4 * q:
                into[rest : 4 * q, h0 : h0 + hs] = raw[i % 2, :hs, rest : 4 * q].T
        else:
            for f in range(4):
                wd[f, h0 : h0 + hs, :] = raw[i % 2, :hs, f * q : (f + 1) * q]

    @pl.loop(0, CHUNKS + BACK)
    def _(t):
        @pl.when(t + AHEAD < CHUNKS)
        def _():
            forward(t + AHEAD, 0)

        @pl.when(t + NEXT < CHUNKS)
        def _():
            forward(t + NEXT, 1)

        @pl.when(t + EARLY < CHUNKS)
        def _():
            dispatch(t + EARLY, 0)
            dispatch(t + EARLY, 1)

        @pl.when(t < CHUNKS)
        def _():
            experts(t)

        @pl.when(t >= BACK)
        def _():
            give_back(t - BACK)

        @pl.when(t >= BACK + ABSORB)
        def _():
            absorb(t - BACK - ABSORB)

    @pl.loop(CHUNKS - ABSORB, CHUNKS)
    def _(ch):
        absorb(ch)

    m1s[...] = macc[1].astype(BF)
    e1s[...] = dot(e_ref[...], m1s[...]).astype(BF)
    hasty = send(e1s, e1r, m_sem.at[2], m_sem.at[3], (away(0), c))
    last = send(m1s, m1r, m_sem.at[0], m_sem.at[1], (away(0), c))
    ends = jnp.dot(e_ref[...].astype(F32), macc[0], preferred_element_type=F32, precision=lax.Precision.HIGHEST)
    kept = dot_nt(e_ref[...], resid_ref[...])
    hasty.wait_recv()
    ends = kept + (ends + e1r[...].astype(F32)).astype(BF).astype(F32)
    ends = jnp.concatenate([ends, jnp.zeros((ends.shape[0], 768 - q), F32)], axis=1)
    piece = lax.broadcasted_iota(jnp.int32, (ends.shape[0], 256), 0) // REQS
    packed = jnp.where(piece == 0, ends[:, :256], jnp.where(piece == 1, ends[:, 256:512], ends[:, 512:]))
    pk[z] = packed.astype(BF)
    more = [send(pk.at[z], pk.at[z], ks.at[o - 1], kr.at[o - 1], (lax.rem(z + o, n), c)) for o in (2, 1, 3)]
    for copy in more:
        copy.wait_recv()
    chip, core = c // 2, c % 2
    own_ends = pltpu.make_async_copy(pk, spread_ref.at[core, chip], own_sem.at[0])
    own_ends.start()

    @pl.loop(1, m // 2)
    def _(j):
        there = (((chip // 4 + j // 4) % 4) * 4 + (chip + j) % 4) * 2 + core
        send(pk, spread_ref.at[core, chip], ss.at[0], sr.at[0], (z, there))

    last.wait_recv()
    moe = (macc[0] + m1r[...].astype(F32)).astype(BF)
    out_ref[...] = (resid_ref[...].astype(F32) + moe.T.astype(F32)).astype(BF)
    own_ends.wait()
    wait_bytes(spread_ref.at[0, pl.ds(0, m // 2 - 1)], sr.at[0])
    pair = send(spread_ref.at[core], spread_ref.at[core], ss.at[1], sr.at[1], (z, chip * 2 + 1 - core))
    last.wait_send()
    hasty.wait_send()
    first.wait_send()
    for copy in more:
        copy.wait_send()

    for r in range(2):
        for ch in range(CHUNKS):
            wait_bytes(xb.at[r, pl.ds(0, span)], zs.at[r, ch])
        for ch in range(CHUNKS - SENDING, CHUNKS):
            wait_bytes(stg.at[r, 0], ds.at[r, ch])
        for ch in range(CHUNKS - RING, CHUNKS):
            wait_bytes(ys.at[r, 0], ps.at[r, ch])
            wait_bytes(yo.at[r, 0], bs.at[r, ch])
    wait_bytes(spread_ref.at[0, pl.ds(0, m // 2 - 1)], ss.at[0])
    pair.wait_send()
    pair.wait_recv()


def experts_call(pick, weigh, choose, moe_in, resid, wg, wu, wd, slots):
    rows, tokens = pick.shape
    q, f = moe_in.shape[0], wg.shape[0]
    columns, groups = rows // slots, wg.shape[1] // q
    span = PER * slots
    dma = lambda *s: pltpu.SemaphoreType.DMA(s)
    big = lambda k: pltpu.VMEM((k, rows, q), BF)
    sending = pltpu.VMEM((2, SENDING, span, q), BF)
    ring = pltpu.VMEM((2, RING, span, q), BF)
    pair = dma(2, CHUNKS)
    return pl.pallas_call(
        functools.partial(expert_kernel, slots),
        out_shape=(
            jax.ShapeDtypeStruct((q, tokens), BF),
            jax.ShapeDtypeStruct((2, columns // 2, groups, 16, 256), BF),
        ),
        in_specs=[ANY, ANY, VMEM] + [ANY] * 5,
        out_specs=(VMEM, ANY),
        scratch_shapes=[
            pltpu.VMEM(pick.shape, BF), pltpu.VMEM(weigh.shape, BF),
            pltpu.VMEM((q, tokens), BF), pltpu.VMEM((q, tokens), BF), dma(4),
            pltpu.VMEM((q, tokens), BF),
            sending, big(4),
            pltpu.VMEM((groups * q, f), BF), pltpu.VMEM((groups * q, f), BF), pltpu.VMEM((groups, f, q), BF),
            pltpu.VMEM((2, 128, groups * q), BF),
            ring, ring, big(2), big(2),
            pltpu.VMEM((2, tokens, q), F32), pltpu.VMEM((tokens, q), BF), pltpu.VMEM((tokens, q), BF),
            pltpu.VMEM((16, q), BF), pltpu.VMEM((16, q), BF),
            pltpu.VMEM((groups, 16, 256), BF),
            dma(2), dma(2),
            pair, pair, pair, pair, pair, pair, pair, pair,
            dma(1), dma(4), dma(3), dma(3), dma(2), dma(2),
        ],
        compiler_params=pltpu.CompilerParams(
            collective_id=2, has_side_effects=True, vmem_limit_bytes=63 * 2**20
        ),
    )(pick, weigh, choose, moe_in, resid, wg, wu, wd)


def head_kernel(spread_ref, gain_ref, vocab_hbm, out_ref, vocab_ref, sem):
    entries = out_ref.shape[0]
    parts = entries // 160
    loads = [
        pltpu.make_async_copy(vocab_hbm.at[pl.ds(i * 160, 160)], vocab_ref.at[pl.ds(i * 160, 160)], sem.at[i])
        for i in range(parts)
    ]
    for load in loads:
        load.start()
    holders, groups, packed, lanes = spread_ref.shape
    rows = out_ref.shape[1]
    width = vocab_ref.shape[1]
    quarter = width // groups
    to = lax.broadcasted_iota(jnp.int32, (rows, holders * packed), 0)
    at = lax.broadcasted_iota(jnp.int32, (rows, holders * packed), 1)
    start = (((to >> 2) & 1) * (holders // 2) + (to >> 3)) * packed + (to & 3)
    select = [jnp.where(at == start + REQS * i, 1.0, 0.0).astype(BF) for i in range(3)]
    pieces = []
    squares = jnp.zeros((rows, 1), F32)
    for f in range(groups):
        block = spread_ref[:, f].reshape(holders * packed, lanes)
        for i in range(3):
            piece = dot(select[i], block)
            squares = squares + jnp.sum(piece * piece, axis=1, keepdims=True)
            pieces.append(piece[:, : min(lanes, quarter - i * lanes)])
    scale = lax.rsqrt(squares / width + epsilon)
    ends = (jnp.concatenate(pieces, axis=1) * scale * gain_ref[...]).astype(BF)
    for i in range(parts):
        loads[i].wait()
        out_ref[i * 160 : (i + 1) * 160] = dot_nt(vocab_ref[i * 160 : (i + 1) * 160], ends)


def head(spread, gain, vocab):
    entries = vocab.shape[0]
    return pl.pallas_call(
        head_kernel,
        out_shape=jax.ShapeDtypeStruct((entries, spread.shape[0] * REQS), F32),
        in_specs=[VMEM, VMEM, ANY],
        out_specs=VMEM,
        scratch_shapes=[pltpu.VMEM(vocab.shape, BF), pltpu.SemaphoreType.DMA((entries // 160,))],
        compiler_params=pltpu.CompilerParams(vmem_limit_bytes=32 * 2**20),
    )(spread, gain, vocab)


def shards(
    hidden, segments, request_adapter, routes, expert_gates, attention_gain, joined_weight, sinks,
    attention_out_weight, joined_down_maps, joined_up_maps, output_down_maps, output_up_maps,
    expert_norm_gain, expert_gate_weight, expert_up_weight, expert_down_weight, closing_gain, vocabulary_weight,
):
    groups, columns = lax.axis_size("dp"), lax.axis_size("expert")
    z, c = lax.axis_index("dp"), lax.axis_index("expert")
    segment_row, adapter_row = segments[0], request_adapter[0]
    tokens, quarter = hidden.shape
    width = quarter * groups
    share = tokens // groups
    aux = jnp.concatenate([routes[0].T.astype(BF), expert_gates[0].T], axis=0)
    aux = jnp.pad(aux, ((0, 16 - 2 * TOP), (0, 128 - share)))
    hid4, aux4 = gather_z(hidden.T, aux)
    rows = hid4.reshape(width, tokens)

    wide = rows.astype(F32)
    mean_square = jnp.mean(wide * wide, axis=0, keepdims=True)
    normed = (wide * lax.rsqrt(mean_square + epsilon) * attention_gain[:, None]).astype(BF)
    ranks = joined_down_maps.shape[1]
    projected = dot_tn(joined_weight.reshape(width, -1), normed)
    low = dot_tn(joined_down_maps, normed).astype(BF)
    request_ids = jnp.arange(REQS, dtype=jnp.int32)
    hits = segment_row[None, :] == request_ids[:, None]
    adapter = jnp.sum(jnp.where(hits, adapter_row[:, None], 0), axis=0)
    mask = adapter[None, :] == (jnp.arange(ranks, dtype=jnp.int32) // ADAPTER_RANK)[:, None]
    low = jnp.where(mask, low, jnp.zeros_like(low))
    projected = projected + adapter_scale * dot_tn(joined_up_maps.reshape(ranks, -1), low)
    counter = jnp.arange(tokens, dtype=jnp.int32)
    starts = jnp.min(jnp.where(hits, counter[None, :], tokens), axis=1)
    positions = counter - jnp.sum(jnp.where(hits, starts[:, None], 0), axis=0)
    half = HEAD_SIZE // 2
    frequency = theta_base ** (-2.0 * jnp.arange(half, dtype=F32) / HEAD_SIZE)
    angles = frequency[:, None] * positions.astype(F32)[None, :]
    cosine, sine = jnp.cos(angles)[None], jnp.sin(angles)[None]
    projected = projected.reshape(QUERY_GROUP + 2, HEAD_SIZE, tokens)
    one, two = projected[: QUERY_GROUP + 1, :half], projected[: QUERY_GROUP + 1, half:]
    turned = jnp.concatenate([one * cosine - two * sine, two * cosine + one * sine], axis=1).astype(BF)
    queries, keys, values = turned[:QUERY_GROUP], turned[QUERY_GROUP], projected[QUERY_GROUP + 1].astype(BF)
    scores = jnp.einsum("ght,hs->gts", queries, keys, preferred_element_type=F32) * HEAD_SIZE ** (-0.5)
    allowed = (segment_row[:, None] == segment_row[None, :]) & (counter[None, :] <= counter[:, None])
    weights = jnp.where(allowed[None], jnp.exp(scores), 0.0)
    totals = jnp.sum(weights, axis=-1, keepdims=True) + jnp.exp(sinks).reshape(QUERY_GROUP, 1, 1)
    probs = (weights / totals).astype(BF)
    blended = jnp.einsum("hs,gts->ght", values, probs, preferred_element_type=F32)
    blended = blended.astype(BF).reshape(QUERY_GROUP * HEAD_SIZE, tokens)

    gain = lax.dynamic_slice_in_dim(expert_norm_gain, z * quarter, quarter)[:, None]
    slots = CAP * groups
    aux = jnp.transpose(aux4[:, :, :share], (1, 0, 2)).reshape(16, tokens).astype(F32)
    targets = shifted(c, jnp.arange(columns, dtype=jnp.int32), 1).astype(F32)
    targets = jnp.broadcast_to(targets[:, None], (columns, 128))
    resid, moe_in, pick, weigh = out_project(
        blended, attention_out_weight.T, output_down_maps, hidden.T, mask.astype(F32), output_up_maps.T, gain,
        aux, targets, slots
    )
    last = jnp.max(jnp.where(hits, counter[None, :], -1), axis=1)
    choose = (counter[None, :] == last[:, None]).astype(BF)
    choose = jnp.concatenate([choose, choose, choose, jnp.zeros_like(choose)], axis=0)

    done, spread = experts_call(
        pick, weigh, choose, moe_in, resid, expert_gate_weight[0].T, expert_up_weight[0].T, expert_down_weight[0], slots
    )

    logits = head(spread.reshape(columns, groups, 16, 256), closing_gain[None, :], vocabulary_weight.T)
    return done.T, logits.T


def solution(mesh):
    in_specs = (
        P("expert", "dp"),
        P("expert", None),
        P("expert", None),
        P("expert", "dp", None),
        P("expert", "dp", None),
        P(),
        P(None, "dp", None),
        P("dp"),
        P("dp", None),
        P(),
        P(None, "dp", None),
        P("dp", None),
        P(None, "dp"),
        P(),
        P("expert", None, "dp"),
        P("expert", None, "dp"),
        P("expert", "dp", None),
        P(),
        P(None, ("dp", "expert")),
    )
    out_specs = (P("expert", "dp"), P(None, ("dp", "expert")))
    return jax.shard_map(shards, mesh=mesh, in_specs=in_specs, out_specs=out_specs, check_vma=False)
```

```python
import functools

import jax
import jax.numpy as jnp
from jax import lax
from jax.experimental import pallas as pl
from jax.experimental.pallas import tpu as pltpu
from jax.sharding import PartitionSpec as P

HEAD_SIZE = 64
QUERY_GROUP = 8
TOP = 4
ADAPTER_RANK = 16
REQS = 4
CAP = 16
CHUNKS = 8
PER = 4
EARLY = 3
AHEAD = 2
NEXT = 1
BACK = 1
ABSORB = 2
SENDING = 4
RING = 3

epsilon = 1e-05
theta_base = 150000.0
adapter_scale = 2.0
glu_alpha = 1.702

MESH = pl.DeviceIdType.MESH
BF = jnp.bfloat16
F32 = jnp.float32
VMEM = pl.BlockSpec(memory_space=pltpu.VMEM)
ANY = pl.BlockSpec(memory_space=pl.ANY)


def dot(a, b):
    return jnp.dot(a, b, preferred_element_type=F32)


def dot_nt(a, b):
    return lax.dot_general(a, b, (((1,), (1,)), ((), ())), preferred_element_type=F32)


def dot_tn(a, b):
    return lax.dot_general(a, b, (((0,), (0,)), ((), ())), preferred_element_type=F32)


def place():
    z, n = lax.axis_index("dp"), lax.axis_size("dp")
    c, m = lax.axis_index("expert"), lax.axis_size("expert")
    return z, n, c, m


def greet_z(offsets):
    z, n, c, _ = place()
    barrier = pltpu.get_barrier_semaphore()
    for o in offsets:
        pl.semaphore_signal(barrier, inc=1, device_id=(lax.rem(z + o, n), c), device_id_type=MESH)
    pl.semaphore_wait(barrier, len(offsets))


def send(src, dst, send_sem, recv_sem, device):
    copy = pltpu.make_async_remote_copy(
        src_ref=src, dst_ref=dst, send_sem=send_sem, recv_sem=recv_sem, device_id=device, device_id_type=MESH
    )
    copy.start()
    return copy


def wait_bytes(ref, sem):
    pltpu.make_async_copy(ref, ref, sem).wait()


def gather_kernel(x_ref, a_ref, xo_ref, ao_ref, ss, rs, local):
    z, n, c, _ = place()
    greet_z((1, 2, 3))
    own = pltpu.make_async_copy(x_ref, xo_ref.at[z], local.at[0])
    own.start()
    own_a = pltpu.make_async_copy(a_ref, ao_ref.at[z], local.at[1])
    own_a.start()
    half = x_ref.shape[0] // 32 * 16
    zu, zd = lax.rem(z + 1, n), lax.rem(z + 3, n)
    up, down, far = (zu, c), (zd, c), (lax.rem(z + 2, n), c)
    lo, hi = pl.ds(0, half), pl.ds(half, x_ref.shape[0] - half)
    copies = [
        send(x_ref.at[lo], xo_ref.at[z, lo], ss.at[0], rs.at[0], up),
        send(x_ref.at[hi], xo_ref.at[z, hi], ss.at[1], rs.at[1], down),
        send(a_ref, ao_ref.at[z], ss.at[6], rs.at[6], up),
        send(a_ref, ao_ref.at[z], ss.at[7], rs.at[7], down),
        send(a_ref, ao_ref.at[z], ss.at[8], rs.at[8], far),
        send(x_ref.at[hi], xo_ref.at[z, hi], ss.at[2], rs.at[2], up),
        send(x_ref.at[lo], xo_ref.at[z, lo], ss.at[3], rs.at[3], down),
    ]
    copies[0].wait_recv()
    copies.append(send(xo_ref.at[zd, lo], xo_ref.at[zd, lo], ss.at[4], rs.at[4], up))
    copies[1].wait_recv()
    copies.append(send(xo_ref.at[zu, hi], xo_ref.at[zu, hi], ss.at[5], rs.at[5], down))
    for copy in copies[2:]:
        copy.wait_recv()
    for copy in copies:
        copy.wait_send()
    own.wait()
    own_a.wait()


def gather_z(hidden, aux):
    n = lax.axis_size("dp")
    return pl.pallas_call(
        gather_kernel,
        out_shape=(
            jax.ShapeDtypeStruct((n,) + hidden.shape, hidden.dtype),
            jax.ShapeDtypeStruct((n,) + aux.shape, aux.dtype),
        ),
        in_specs=[VMEM, VMEM],
        out_specs=(VMEM, VMEM),
        scratch_shapes=[
            pltpu.SemaphoreType.DMA((9,)),
            pltpu.SemaphoreType.DMA((9,)),
            pltpu.SemaphoreType.DMA((2,)),
        ],
        compiler_params=pltpu.CompilerParams(
            collective_id=0, has_side_effects=True, vmem_limit_bytes=32 * 2**20
        ),
    )(hidden, aux)


def out_kernel(
    b_ref, wo_hbm, odm_hbm, hid_hbm, mask_ref, oum_hbm, gain_ref, aux_ref, target_ref,
    resid_ref, moe_ref, pick_ref, weigh_ref,
    wo_ref, odm_ref, hid_ref, oum_ref, low_snd, low_rcv, far, passed, snd, rcv, st_snd, st_rcv, fetch, ss, rs,
):
    z, n, c, _ = place()
    loads = [
        pltpu.make_async_copy(src, dst, fetch.at[i])
        for i, (src, dst) in enumerate(
            ((wo_hbm, wo_ref), (odm_hbm, odm_ref), (hid_hbm, hid_ref), (oum_hbm, oum_ref))
        )
    ]
    for load in loads:
        load.start()
    quarter = hid_ref.shape[0]
    half = quarter // 32 * 16
    lo, hi = pl.ds(0, half), pl.ds(half, quarter - half)
    zu, zf, zd = lax.rem(z + 1, n), lax.rem(z + 2, n), lax.rem(z + 3, n)
    up, down = (zu, c), (zd, c)
    blended = b_ref[...]

    def part(q):
        return dot(wo_ref[pl.ds(pl.multiple_of(q * quarter, 16), quarter)], blended)

    greet_z((1, 2, 3))
    loads[0].wait()
    far[...] = part(zf).astype(BF)
    relays = [
        send(far.at[lo], passed.at[lo], ss.at[3], rs.at[3], up),
        send(far.at[hi], passed.at[hi], ss.at[4], rs.at[4], down),
    ]
    above, below = part(zu), part(zd)
    snd[0, half:] = above[half:].astype(BF)
    snd[1, :half] = below[:half].astype(BF)
    shares = [
        send(snd.at[0, hi], rcv.at[0, hi], ss.at[5], rs.at[5], up),
        send(snd.at[1, lo], rcv.at[1, lo], ss.at[6], rs.at[6], down),
    ]
    loads[1].wait()
    low = dot_tn(odm_ref[...], blended).astype(BF)
    low_snd[...] = low
    lows = [
        send(low_snd, low_rcv.at[o - 1], ss.at[o - 1], rs.at[o - 1], (lax.rem(z + o, n), c)) for o in (2, 1, 3)
    ]
    relays[0].wait_recv()
    snd[0, :half] = (above[:half] + passed[:half].astype(F32)).astype(BF)
    shares.append(send(snd.at[0, lo], rcv.at[0, lo], ss.at[7], rs.at[7], up))
    relays[1].wait_recv()
    snd[1, half:] = (below[half:] + passed[half:].astype(F32)).astype(BF)
    shares.append(send(snd.at[1, hi], rcv.at[1, hi], ss.at[8], rs.at[8], down))
    for load in loads[2:]:
        load.wait()
    total = hid_ref[...].astype(F32) + part(z)

    blocks, tokens = target_ref.shape[0], hid_ref.shape[1]
    slots = pick_ref.shape[0] // blocks
    aux = aux_ref[...]
    hit = jnp.zeros((blocks, tokens), F32)
    gate = jnp.zeros((blocks, tokens), F32)
    for k in range(TOP):
        same = aux[k : k + 1] == target_ref[:, :1]
        hit = jnp.where(same, 1.0, hit)
        gate = jnp.where(same, aux[TOP + k : TOP + k + 1], gate)
    before = lax.broadcasted_iota(jnp.int32, (tokens, tokens), 0) < lax.broadcasted_iota(jnp.int32, (tokens, tokens), 1)
    rank = jnp.where(hit > 0.5, dot(hit.astype(BF), before.astype(F32).astype(BF)), -1.0)
    ids = lax.broadcasted_iota(jnp.int32, (slots, tokens), 0).astype(F32)
    for j in range(blocks):
        here = ids == rank[j : j + 1]
        pick_ref[j * slots : (j + 1) * slots] = jnp.where(here, 1.0, 0.0).astype(BF)
        weigh_ref[j * slots : (j + 1) * slots] = jnp.where(here, gate[j : j + 1], 0.0).astype(BF)

    for copy in lows:
        copy.wait_recv()
    low_sum = low.astype(F32)
    for k in range(3):
        low_sum = low_sum + low_rcv[k].astype(F32)
    picked = (low_sum * mask_ref[...]).astype(BF)
    total = total + adapter_scale * dot(oum_ref[...], picked)
    for copy in shares:
        copy.wait_recv()
    total = total + rcv[0].astype(F32) + rcv[1].astype(F32)
    resid = total.astype(BF)
    resid_ref[...] = resid
    wide = resid.astype(F32)
    sums = jnp.sum(wide * wide, axis=0, keepdims=True)
    st_snd[...] = jnp.broadcast_to(sums, st_snd.shape)
    more = []
    for o in (2, 1, 3):
        more.append(send(st_snd, st_rcv.at[o - 1], ss.at[o + 8], rs.at[o + 8], (lax.rem(z + o, n), c)))
    for copy in more:
        copy.wait_recv()
    every = st_snd[...] + st_rcv[0] + st_rcv[1] + st_rcv[2]
    scale = lax.rsqrt(every / (4.0 * quarter) + epsilon)
    moe_ref[...] = (wide * scale[:1] * gain_ref[...]).astype(BF)
    for copy in relays + shares + lows + more:
        copy.wait_send()


def out_project(blended, wo, odm, hidden, mask, oum, gain, aux, targets, slots):
    q, rows = hidden.shape
    table = jax.ShapeDtypeStruct((targets.shape[0] * slots, rows), BF)
    n = 3
    return pl.pallas_call(
        out_kernel,
        out_shape=(jax.ShapeDtypeStruct((q, rows), BF), jax.ShapeDtypeStruct((q, rows), BF), table, table),
        in_specs=[VMEM, ANY, ANY, ANY, VMEM, ANY, VMEM, VMEM, VMEM],
        out_specs=(VMEM,) * 4,
        scratch_shapes=[
            pltpu.VMEM(wo.shape, BF),
            pltpu.VMEM(odm.shape, BF),
            pltpu.VMEM(hidden.shape, BF),
            pltpu.VMEM(oum.shape, BF),
            pltpu.VMEM(mask.shape, BF),
            pltpu.VMEM((n,) + mask.shape, BF),
            pltpu.VMEM((q, rows), BF),
            pltpu.VMEM((q, rows), BF),
            pltpu.VMEM((2, q, rows), BF),
            pltpu.VMEM((2, q, rows), BF),
            pltpu.VMEM((8, rows), F32),
            pltpu.VMEM((n, 8, rows), F32),
            pltpu.SemaphoreType.DMA((4,)),
            pltpu.SemaphoreType.DMA((12,)),
            pltpu.SemaphoreType.DMA((12,)),
        ],
        compiler_params=pltpu.CompilerParams(
            collective_id=1, has_side_effects=True, vmem_limit_bytes=48 * 2**20
        ),
    )(blended, wo, odm, hidden, mask, oum, gain, aux, targets)


def shift_of(j):
    s, dx = j // PER, j % PER
    return dx, (dx + s // 2) % 4, s % 2


def shifted(c, j, way):
    dx, dy, dk = shift_of(j)
    x, y, k = c // 8, (c // 2) % 4, c % 2
    return (((x + way * dx + 4) % 4) * 4 + (y + way * dy + 4) % 4) * 2 + (k + dk) % 2


def expert_kernel(
    slots, d_ref, g_ref, e_ref, mi_ref, resid_ref, wg_hbm, wu_hbm, wd_hbm,
    out_ref, spread_ref,
    mi_nb, stg, xb, wg, wu, wd, raw, yo, ys, yr, ans, macc, m1s, m1r, e1s, e1r, pk,
    w_sem, mi_sem, ds, dr, zs, zr, ps, pr, bs, br, own_sem, m_sem, ks, kr, ss, sr,
):
    z, n, c, m = place()
    span = PER * slots
    q = mi_ref.shape[0]

    def step(ch):
        return 1 + 2 * lax.rem(c + ch, 2)

    def near(ch):
        return lax.rem(z + step(ch), n)

    def away(ch):
        return lax.rem(z + 4 - step(ch), n)

    def quarters(ch):
        return z, away(ch), near(ch), lax.rem(z + 2, n)

    barrier = pltpu.get_barrier_semaphore()

    @pl.loop(1, m)
    def _(j):
        pl.semaphore_signal(barrier, inc=1, device_id=(z, lax.rem(c + j, m)), device_id_type=MESH)

    for o in (1, 2, 3):
        pl.semaphore_signal(barrier, inc=1, device_id=(lax.rem(z + o, n), c), device_id_type=MESH)
    pl.semaphore_wait(barrier, m + 2)
    first = send(mi_ref, mi_nb, mi_sem.at[0], mi_sem.at[1], (near(0), c))

    def block(j):
        return pl.ds(pl.multiple_of(j * slots, slots), slots)

    def chunk(ch):
        return pl.ds(pl.multiple_of(ch * span, span), span)

    def sent_in_plane(ring, sem, r, ch):
        @pl.when(ch == 0)
        def _():
            wait_bytes(ring.at[r, 0, pl.ds(0, span - slots)], sem.at[r, ch])

        @pl.when(ch != 0)
        def _():
            wait_bytes(ring.at[r, 0], sem.at[r, ch])

    def others(ch):
        return 1 - (ch + CHUNKS - 1) // CHUNKS

    def dispatch(ch, r):
        slot = lax.rem(ch, SENDING)
        source = mi_ref if r == 0 else mi_nb

        @pl.when(ch >= SENDING)
        def _():
            sent_in_plane(stg, ds, r, ch - SENDING)

        stg[r, slot] = dot_nt(d_ref[chunk(ch)], source[...]).astype(BF)

        @pl.loop(others(ch), PER)
        def _(a):
            j = ch * PER + a
            send(stg.at[r, slot, block(a)], xb.at[r, block(j)], ds.at[r, ch], dr.at[r, ch], (z, shifted(c, j, 1)))

        @pl.when(ch == 0)
        def _():
            xb[r, :slots] = stg[r, 0, :slots]

    def came_in_plane(buffer, sem, r, ch):
        @pl.when(ch == 0)
        def _():
            wait_bytes(buffer.at[r, pl.ds(slots, span - slots)], sem.at[r, ch])

        @pl.when(ch != 0)
        def _():
            wait_bytes(buffer.at[r, chunk(ch)], sem.at[r, ch])

    def forward(ch, r):
        came_in_plane(xb, dr, r, ch)
        there = (away(ch), near(ch))[r]
        send(xb.at[r, chunk(ch)], xb.at[r + 2, chunk(ch)], zs.at[r, ch], zr.at[r, ch], (there, c))

    def experts(ch):
        slot = lax.rem(ch, RING)
        at = chunk(ch)
        names = quarters(ch)

        def rows_of(r):
            return pl.ds(pl.multiple_of(names[r] * q, 16), q)

        for r in range(2):
            wait_bytes(xb.at[r + 2, at], zr.at[r, ch])

            @pl.when(ch >= RING)
            def _():
                wait_bytes(ys.at[r, 0], ps.at[r, ch - RING])
                sent_in_plane(yo, bs, r, ch - RING)

        gate = dot(xb[0, at], wg[rows_of(0)])
        for r in range(1, 4):
            gate = gate + dot(xb[r, at], wg[rows_of(r)])
        lift = dot(xb[0, at], wu[rows_of(0)])
        for r in range(1, 4):
            lift = lift + dot(xb[r, at], wu[rows_of(r)])
        act = (gate * jax.nn.sigmoid(glu_alpha * gate) * (lift + 1.0)).astype(BF)
        for r in range(2):
            ys[r, slot] = dot(act, wd[names[r + 2]]).astype(BF)
            send(ys.at[r, slot], yr.at[r, at], ps.at[r, ch], pr.at[r, ch], ((near(ch), away(ch))[r], c))
        for r in range(2):
            yo[r, slot] = dot(act, wd[names[r]]).astype(BF)

    def give_back(ch):
        slot = lax.rem(ch, RING)
        for r in range(2):
            wait_bytes(yr.at[r, chunk(ch)], pr.at[r, ch])
            yo[r, slot] = (yo[r, slot].astype(F32) + yr[r, chunk(ch)].astype(F32)).astype(BF)

            @pl.loop(others(ch), PER)
            def _(a):
                j = ch * PER + a
                send(yo.at[r, slot, block(a)], ans.at[r, block(j)], bs.at[r, ch], br.at[r, ch], (z, shifted(c, j, -1)))

            @pl.when(ch == 0)
            def _():
                ans[r, :slots] = yo[r, 0, :slots]

    def absorb(ch):
        for r in (1, 0):
            came_in_plane(ans, br, r, ch)
            macc[r] += dot_tn(g_ref[chunk(ch)], ans[r, chunk(ch)])

    steps = [(w, h0, min(128, q - h0)) for w in range(3) for h0 in range(0, q, 128)]

    def fetch(i):
        w, h0, hs = steps[i]
        return pltpu.make_async_copy(
            (wg_hbm, wu_hbm, wd_hbm)[w].at[pl.ds(h0, hs)], raw.at[i % 2, pl.ds(0, hs)], w_sem.at[i % 2]
        )

    fetch(0).start()

    head = 2

    @pl.loop(0, head)
    def _(ch):
        dispatch(ch, 0)

    macc[...] = jnp.zeros_like(macc)
    first.wait_recv()

    @pl.loop(0, head)
    def _(ch):
        dispatch(ch, 1)

    @pl.loop(head, EARLY)
    def _(ch):
        dispatch(ch, 0)
        dispatch(ch, 1)

    for i, (w, h0, hs) in enumerate(steps):
        if i == len(steps) // 3:

            @pl.loop(0, AHEAD)
            def _(ch):
                forward(ch, 0)

        if i == 2 * len(steps) // 3:

            @pl.loop(0, NEXT)
            def _(ch):
                forward(ch, 1)

        if i + 1 < len(steps):
            fetch(i + 1).start()
        fetch(i).wait()
        if w < 2:
            into = (wg, wu)[w]
            whole = 4 * q // 128

            @pl.loop(0, whole)
            def _(b):
                lanes = pl.ds(pl.multiple_of(b * 128, 128), 128)
                into[lanes, h0 : h0 + hs] = raw[i % 2, :hs, lanes].T

            rest = whole * 128
            if rest < 4 * q:
                into[rest : 4 * q, h0 : h0 + hs] = raw[i % 2, :hs, rest : 4 * q].T
        else:
            for f in range(4):
                wd[f, h0 : h0 + hs, :] = raw[i % 2, :hs, f * q : (f + 1) * q]

    @pl.loop(0, CHUNKS + BACK)
    def _(t):
        @pl.when(t + AHEAD < CHUNKS)
        def _():
            forward(t + AHEAD, 0)

        @pl.when(t + NEXT < CHUNKS)
        def _():
            forward(t + NEXT, 1)

        @pl.when(t + EARLY < CHUNKS)
        def _():
            dispatch(t + EARLY, 0)
            dispatch(t + EARLY, 1)

        @pl.when(t < CHUNKS)
        def _():
            experts(t)

        @pl.when(t >= BACK)
        def _():
            give_back(t - BACK)

        @pl.when(t >= BACK + ABSORB)
        def _():
            absorb(t - BACK - ABSORB)

    @pl.loop(CHUNKS - ABSORB, CHUNKS)
    def _(ch):
        absorb(ch)

    m1s[...] = macc[1].astype(BF)
    e1s[...] = dot(e_ref[...], m1s[...]).astype(BF)
    hasty = send(e1s, e1r, m_sem.at[2], m_sem.at[3], (away(0), c))
    last = send(m1s, m1r, m_sem.at[0], m_sem.at[1], (away(0), c))
    ends = jnp.dot(e_ref[...].astype(F32), macc[0], preferred_element_type=F32, precision=lax.Precision.HIGHEST)
    kept = dot_nt(e_ref[...], resid_ref[...])
    hasty.wait_recv()
    ends = kept + (ends + e1r[...].astype(F32)).astype(BF).astype(F32)
    ends = jnp.concatenate([ends, jnp.zeros((ends.shape[0], 768 - q), F32)], axis=1)
    piece = lax.broadcasted_iota(jnp.int32, (ends.shape[0], 256), 0) // REQS
    packed = jnp.where(piece == 0, ends[:, :256], jnp.where(piece == 1, ends[:, 256:512], ends[:, 512:]))
    pk[z] = packed.astype(BF)
    more = [send(pk.at[z], pk.at[z], ks.at[o - 1], kr.at[o - 1], (lax.rem(z + o, n), c)) for o in (2, 1, 3)]
    for copy in more:
        copy.wait_recv()
    chip, core = c // 2, c % 2
    own_ends = pltpu.make_async_copy(pk, spread_ref.at[core, chip], own_sem.at[0])
    own_ends.start()

    @pl.loop(1, m // 2)
    def _(j):
        there = (((chip // 4 + j // 4) % 4) * 4 + (chip + j) % 4) * 2 + core
        send(pk, spread_ref.at[core, chip], ss.at[0], sr.at[0], (z, there))

    last.wait_recv()
    moe = (macc[0] + m1r[...].astype(F32)).astype(BF)
    out_ref[...] = (resid_ref[...].astype(F32) + moe.T.astype(F32)).astype(BF)
    own_ends.wait()
    wait_bytes(spread_ref.at[0, pl.ds(0, m // 2 - 1)], sr.at[0])
    pair = send(spread_ref.at[core], spread_ref.at[core], ss.at[1], sr.at[1], (z, chip * 2 + 1 - core))
    last.wait_send()
    hasty.wait_send()
    first.wait_send()
    for copy in more:
        copy.wait_send()

    for r in range(2):
        for ch in range(CHUNKS):
            wait_bytes(xb.at[r, pl.ds(0, span)], zs.at[r, ch])
        for ch in range(CHUNKS - SENDING, CHUNKS):
            wait_bytes(stg.at[r, 0], ds.at[r, ch])
        for ch in range(CHUNKS - RING, CHUNKS):
            wait_bytes(ys.at[r, 0], ps.at[r, ch])
            wait_bytes(yo.at[r, 0], bs.at[r, ch])
    wait_bytes(spread_ref.at[0, pl.ds(0, m // 2 - 1)], ss.at[0])
    pair.wait_send()
    pair.wait_recv()


def experts_call(pick, weigh, choose, moe_in, resid, wg, wu, wd, slots):
    rows, tokens = pick.shape
    q, f = moe_in.shape[0], wg.shape[0]
    columns, groups = rows // slots, wg.shape[1] // q
    span = PER * slots
    dma = lambda *s: pltpu.SemaphoreType.DMA(s)
    big = lambda k: pltpu.VMEM((k, rows, q), BF)
    sending = pltpu.VMEM((2, SENDING, span, q), BF)
    ring = pltpu.VMEM((2, RING, span, q), BF)
    pair = dma(2, CHUNKS)
    return pl.pallas_call(
        functools.partial(expert_kernel, slots),
        out_shape=(
            jax.ShapeDtypeStruct((q, tokens), BF),
            jax.ShapeDtypeStruct((2, columns // 2, groups, 16, 256), BF),
        ),
        in_specs=[VMEM] * 5 + [ANY] * 3,
        out_specs=(VMEM, ANY),
        scratch_shapes=[
            pltpu.VMEM((q, tokens), BF),
            sending, big(4),
            pltpu.VMEM((groups * q, f), BF), pltpu.VMEM((groups * q, f), BF), pltpu.VMEM((groups, f, q), BF),
            pltpu.VMEM((2, 128, groups * q), BF),
            ring, ring, big(2), big(2),
            pltpu.VMEM((2, tokens, q), F32), pltpu.VMEM((tokens, q), BF), pltpu.VMEM((tokens, q), BF),
            pltpu.VMEM((16, q), BF), pltpu.VMEM((16, q), BF),
            pltpu.VMEM((groups, 16, 256), BF),
            dma(2), dma(2),
            pair, pair, pair, pair, pair, pair, pair, pair,
            dma(1), dma(4), dma(3), dma(3), dma(2), dma(2),
        ],
        compiler_params=pltpu.CompilerParams(
            collective_id=2, has_side_effects=True, vmem_limit_bytes=63 * 2**20
        ),
    )(pick, weigh, choose, moe_in, resid, wg, wu, wd)


def head_kernel(spread_ref, gain_ref, vocab_hbm, out_ref, vocab_ref, sem):
    entries = out_ref.shape[0]
    parts = entries // 160
    loads = [
        pltpu.make_async_copy(vocab_hbm.at[pl.ds(i * 160, 160)], vocab_ref.at[pl.ds(i * 160, 160)], sem.at[i])
        for i in range(parts)
    ]
    for load in loads:
        load.start()
    holders, groups, packed, lanes = spread_ref.shape
    rows = out_ref.shape[1]
    width = vocab_ref.shape[1]
    quarter = width // groups
    to = lax.broadcasted_iota(jnp.int32, (rows, holders * packed), 0)
    at = lax.broadcasted_iota(jnp.int32, (rows, holders * packed), 1)
    start = (((to >> 2) & 1) * (holders // 2) + (to >> 3)) * packed + (to & 3)
    select = [jnp.where(at == start + REQS * i, 1.0, 0.0).astype(BF) for i in range(3)]
    pieces = []
    squares = jnp.zeros((rows, 1), F32)
    for f in range(groups):
        block = spread_ref[:, f].reshape(holders * packed, lanes)
        for i in range(3):
            piece = dot(select[i], block)
            squares = squares + jnp.sum(piece * piece, axis=1, keepdims=True)
            pieces.append(piece[:, : min(lanes, quarter - i * lanes)])
    scale = lax.rsqrt(squares / width + epsilon)
    ends = (jnp.concatenate(pieces, axis=1) * scale * gain_ref[...]).astype(BF)
    for i in range(parts):
        loads[i].wait()
        out_ref[i * 160 : (i + 1) * 160] = dot_nt(vocab_ref[i * 160 : (i + 1) * 160], ends)


def head(spread, gain, vocab):
    entries = vocab.shape[0]
    return pl.pallas_call(
        head_kernel,
        out_shape=jax.ShapeDtypeStruct((entries, spread.shape[0] * REQS), F32),
        in_specs=[VMEM, VMEM, ANY],
        out_specs=VMEM,
        scratch_shapes=[pltpu.VMEM(vocab.shape, BF), pltpu.SemaphoreType.DMA((entries // 160,))],
        compiler_params=pltpu.CompilerParams(vmem_limit_bytes=32 * 2**20),
    )(spread, gain, vocab)


def shards(
    hidden, segments, request_adapter, routes, expert_gates, attention_gain, joined_weight, sinks,
    attention_out_weight, joined_down_maps, joined_up_maps, output_down_maps, output_up_maps,
    expert_norm_gain, expert_gate_weight, expert_up_weight, expert_down_weight, closing_gain, vocabulary_weight,
):
    groups, columns = lax.axis_size("dp"), lax.axis_size("expert")
    z, c = lax.axis_index("dp"), lax.axis_index("expert")
    segment_row, adapter_row = segments[0], request_adapter[0]
    tokens, quarter = hidden.shape
    width = quarter * groups
    share = tokens // groups
    aux = jnp.concatenate([routes[0].T.astype(BF), expert_gates[0].T], axis=0)
    aux = jnp.pad(aux, ((0, 16 - 2 * TOP), (0, 128 - share)))
    hid4, aux4 = gather_z(hidden.T, aux)
    rows = hid4.reshape(width, tokens)

    wide = rows.astype(F32)
    mean_square = jnp.mean(wide * wide, axis=0, keepdims=True)
    normed = (wide * lax.rsqrt(mean_square + epsilon) * attention_gain[:, None]).astype(BF)
    ranks = joined_down_maps.shape[1]
    projected = dot_tn(joined_weight.reshape(width, -1), normed)
    low = dot_tn(joined_down_maps, normed).astype(BF)
    request_ids = jnp.arange(REQS, dtype=jnp.int32)
    hits = segment_row[None, :] == request_ids[:, None]
    adapter = jnp.sum(jnp.where(hits, adapter_row[:, None], 0), axis=0)
    mask = adapter[None, :] == (jnp.arange(ranks, dtype=jnp.int32) // ADAPTER_RANK)[:, None]
    low = jnp.where(mask, low, jnp.zeros_like(low))
    projected = projected + adapter_scale * dot_tn(joined_up_maps.reshape(ranks, -1), low)
    counter = jnp.arange(tokens, dtype=jnp.int32)
    starts = jnp.min(jnp.where(hits, counter[None, :], tokens), axis=1)
    positions = counter - jnp.sum(jnp.where(hits, starts[:, None], 0), axis=0)
    half = HEAD_SIZE // 2
    frequency = theta_base ** (-2.0 * jnp.arange(half, dtype=F32) / HEAD_SIZE)
    angles = frequency[:, None] * positions.astype(F32)[None, :]
    cosine, sine = jnp.cos(angles)[None], jnp.sin(angles)[None]
    projected = projected.reshape(QUERY_GROUP + 2, HEAD_SIZE, tokens)
    one, two = projected[: QUERY_GROUP + 1, :half], projected[: QUERY_GROUP + 1, half:]
    turned = jnp.concatenate([one * cosine - two * sine, two * cosine + one * sine], axis=1).astype(BF)
    queries, keys, values = turned[:QUERY_GROUP], turned[QUERY_GROUP], projected[QUERY_GROUP + 1].astype(BF)
    scores = jnp.einsum("ght,hs->gts", queries, keys, preferred_element_type=F32) * HEAD_SIZE ** (-0.5)
    allowed = (segment_row[:, None] == segment_row[None, :]) & (counter[None, :] <= counter[:, None])
    weights = jnp.where(allowed[None], jnp.exp(scores), 0.0)
    totals = jnp.sum(weights, axis=-1, keepdims=True) + jnp.exp(sinks).reshape(QUERY_GROUP, 1, 1)
    probs = (weights / totals).astype(BF)
    blended = jnp.einsum("hs,gts->ght", values, probs, preferred_element_type=F32)
    blended = blended.astype(BF).reshape(QUERY_GROUP * HEAD_SIZE, tokens)

    gain = lax.dynamic_slice_in_dim(expert_norm_gain, z * quarter, quarter)[:, None]
    slots = CAP * groups
    aux = jnp.transpose(aux4[:, :, :share], (1, 0, 2)).reshape(16, tokens).astype(F32)
    targets = shifted(c, jnp.arange(columns, dtype=jnp.int32), 1).astype(F32)
    targets = jnp.broadcast_to(targets[:, None], (columns, 128))
    resid, moe_in, pick, weigh = out_project(
        blended, attention_out_weight.T, output_down_maps, hidden.T, mask.astype(F32), output_up_maps.T, gain,
        aux, targets, slots
    )
    last = jnp.max(jnp.where(hits, counter[None, :], -1), axis=1)
    choose = (counter[None, :] == last[:, None]).astype(BF)
    choose = jnp.concatenate([choose, choose, choose, jnp.zeros_like(choose)], axis=0)

    done, spread = experts_call(
        pick, weigh, choose, moe_in, resid, expert_gate_weight[0].T, expert_up_weight[0].T, expert_down_weight[0], slots
    )

    logits = head(spread.reshape(columns, groups, 16, 256), closing_gain[None, :], vocabulary_weight.T)
    return done.T, logits.T


def solution(mesh):
    in_specs = (
        P("expert", "dp"),
        P("expert", None),
        P("expert", None),
        P("expert", "dp", None),
        P("expert", "dp", None),
        P(),
        P(None, "dp", None),
        P("dp"),
        P("dp", None),
        P(),
        P(None, "dp", None),
        P("dp", None),
        P(None, "dp"),
        P(),
        P("expert", None, "dp"),
        P("expert", None, "dp"),
        P("expert", "dp", None),
        P(),
        P(None, ("dp", "expert")),
    )
    out_specs = (P("expert", "dp"), P(None, ("dp", "expert")))
    return jax.shard_map(shards, mesh=mesh, in_specs=in_specs, out_specs=out_specs, check_vma=False)
```
